32 devices in a mesh: groups: 2 (over x), seq: 16 (over z, y, core).
Axes of the slice: x: 2, y: 2, z: 4, core: 2. Of those that a mesh axis runs over, the one named last changes fastest.
Arguments:
- latents: bfloat16 [2304, 128, 512], P(('groups', 'seq')), parts along dimension 0, may hold values from -6 to 6
- queries: bfloat16 [96, 4, 8192], P(('groups', 'seq')), parts along dimension 0, may hold values from -240 to 240
- new_latents: bfloat16 [96, 4, 512], P(('groups', 'seq')), parts along dimension 0, may hold values from -6 to 6
- up_proj: bfloat16 [2, 256, 1024], P(None, 'seq'), may hold values from -0.375 to 0.375
- lengths: int32 [96], P('groups'), parts along dimension 0, may hold values from 1152 to 3072, as said below
- place: int32 [96], P('groups'), parts along dimension 0, may hold values from 0 to 47, as said below
- block_src: int32 [96, 24], P('groups'), parts along dimension 0, may hold values from 0 to 15, as said below
- block_slot: int32 [96, 24], P('groups'), parts along dimension 0, may hold values from 0 to 71
Outputs:
- attn_out: bfloat16 [96, 4, 8192], P(('groups', 'seq')), parts along dimension 0
The draws below stay inside these ranges and needn't reach their ends.
There are 2 independent parts, one for each index of `groups`. The reference program is written for one: setup_inputs(seed, part) draws one part's arguments, and reference() takes and returns one part's arrays. A program takes and returns all parts, laid end to end along the dimension named above; an argument that names none is the same for every part. Nothing has to cross between parts.
Inputs may be any that keep to these rules, and one draw needn't show every extreme that they name: Block j of request r lies in row block_src[r, j] * 72 + block_slot[r, j] of latents; no two blocks of the part share a row; of the blocks of the requests that one device decodes, at most 5 lie on any one device. Only blocks j with j * 128 < lengths[r] are read. `place`: each decode row is taken by exactly one request; device i decodes the rows i * 3 to (i + 1) * 3 - 1. `lengths`: some request has exactly 3072 cached tokens.
All inputs are finite; a program needn't handle non-finite values.
Results may differ from the reference program's by a relative error of at most 0.012.
The reference program's roundings to bfloat16 on the way count: a program that leaves them out, or rounds other values in their place, can miss the bound.
Values may be sent and summed in bfloat16 or wider, within the bound.
A program may use at most 128 MiB of HBM per device.

```python
import jax
import jax.numpy as jnp
from jax import lax

HQ = 64
HK = 8
HD = 128
R = 256
BLOCK = 128
MAXB = 24
STEPS = 4
BDEV = 3
B = 48
SLOTS = 72
CAP = 5
N_SEQ = 16


def layout(key):
    keys_list = jax.random.split(key, 5)
    place = jax.random.permutation(keys_list[0], B).astype(jnp.int32)
    request_of = jnp.zeros((B,), jnp.int32).at[place].set(jnp.arange(B, dtype=jnp.int32))
    virtual = jax.random.permutation(keys_list[1], N_SEQ * CAP).astype(jnp.int32)[:SLOTS]
    spread = jax.random.permutation(keys_list[2], N_SEQ).astype(jnp.int32)
    shuffle = jax.random.permutation(keys_list[3], SLOTS).astype(jnp.int32)
    rows = jnp.arange(B, dtype=jnp.int32)
    decoder = rows // BDEV
    local_index = rows % BDEV
    position = local_index[:, None] * MAXB + jnp.arange(MAXB, dtype=jnp.int32)[None, :]
    chosen = virtual[position]
    holder = spread[(chosen % N_SEQ + decoder[:, None]) % N_SEQ]
    slot_ids = shuffle[(position + holder) % SLOTS]
    sources = jnp.zeros((B, MAXB), jnp.int32).at[request_of].set(holder)
    slots = jnp.zeros((B, MAXB), jnp.int32).at[request_of].set(slot_ids)
    lengths = jax.random.randint(keys_list[4], (B,), MAXB * BLOCK * 3 // 8, MAXB * BLOCK + 1).astype(jnp.int32)
    lengths = lengths.at[0].set(MAXB * BLOCK)
    return (lengths, place, sources, slots)


def draw_lengths(key, part):
    shared = layout(key)
    return shared[0]


def draw_place(key, part):
    shared = layout(key)
    return shared[1]


def draw_block_src(key, part):
    shared = layout(key)
    return shared[2]


def draw_block_slot(key, part):
    shared = layout(key)
    return shared[3]


def draw_queries(key, part):
    key = jax.random.fold_in(key, 7)
    first = jax.random.fold_in(key, 0)
    base = jnp.clip(jax.random.normal(first, (B, STEPS, HQ, HD), jnp.float32), -6.0, 6.0)
    return base.reshape(B, STEPS, HQ * HD).astype(jnp.bfloat16)


def level_of(rng, dims, cuts, low, top_value):
    factor_of = 1.0
    for dim, parts in cuts:
        steps = jax.random.uniform(jax.random.fold_in(jax.random.fold_in(rng, 6), dim), (parts,), jnp.float32, low / len(cuts), top_value / len(cuts))
        factor_of = factor_of * jnp.repeat(jnp.exp(steps), dims[dim] // parts).reshape((-1,) + (1,) * (len(dims) - 1 - dim))
    return factor_of


def normal_values(rng, dims, scale, most, pieces=(), kind=jnp.bfloat16):
    entries = jax.random.normal(rng, dims, jnp.float32) * scale
    if len(pieces) > 0:
        entries = level_of(rng, dims, pieces, -0.22, 0.18) * entries
    return jnp.clip(entries, min=-most, max=most).astype(kind)


def setup_inputs(seed: int = 0, part: int = 0) -> dict:
    streams_of = jax.random.split(jax.random.key(seed), 9)
    part_splits = jax.random.split(jax.random.fold_in(streams_of[8], part), 9)
    latents = normal_values(part_splits[0], (N_SEQ * SLOTS, BLOCK, 2 * R), 1.0, 6.0, ((0, 16),))
    queries = draw_queries(jax.random.fold_in(jax.random.fold_in(streams_of[8], part), 71), part)
    new_latents = normal_values(part_splits[2], (B, STEPS, 2 * R), 1.0, 6.0, ((0, 16),))
    up_proj = normal_values(streams_of[3], (2, R, HK * HD), R ** -0.5, 0.375, ((1, 16),))
    lengths = draw_lengths(jax.random.fold_in(jax.random.fold_in(streams_of[8], part), 71), part)
    place = draw_place(jax.random.fold_in(jax.random.fold_in(streams_of[8], part), 71), part)
    block_src = draw_block_src(jax.random.fold_in(jax.random.fold_in(streams_of[8], part), 71), part)
    block_slot = draw_block_slot(jax.random.fold_in(jax.random.fold_in(streams_of[8], part), 71), part)
    return {"latents": latents, "queries": queries, "new_latents": new_latents, "up_proj": up_proj, "lengths": lengths, "place": place, "block_src": block_src, "block_slot": block_slot}


def rounded(values):
    return lax.optimization_barrier(values.astype(jnp.bfloat16)).astype(jnp.float32)


def reference(latents, queries, new_latents, up_proj, lengths, place, block_src, block_slot):
    request_of = jnp.zeros((B,), jnp.int32).at[place].set(jnp.arange(B, dtype=jnp.int32))
    up_key = up_proj[0].astype(jnp.float32)
    up_value = up_proj[1].astype(jnp.float32)
    context = MAXB * BLOCK
    scale = HD ** -0.5
    group = HQ // HK
    positions = jnp.arange(context + STEPS, dtype=jnp.int32)
    step_ids = jnp.arange(STEPS, dtype=jnp.int32)

    def decode_row(row_index):
        request = request_of[row_index]
        storage = (block_src[request] * SLOTS + block_slot[request]).astype(jnp.int32)
        blocks = jnp.take(latents, storage, axis=0).reshape(context, 2 * R)
        stacked = jnp.concatenate([blocks, new_latents[row_index]], axis=0).astype(jnp.float32)
        key_rows = rounded(jnp.dot(stacked[:, :R], up_key))
        value_rows = rounded(jnp.dot(stacked[:, R:], up_value))
        query_heads = queries[row_index].astype(jnp.float32).reshape(STEPS, HK, group, HD)
        scores = jnp.einsum('sgjd,tgd->gjst', query_heads, key_rows.reshape(-1, HK, HD)) * scale
        visible = jnp.where(positions[None, :] < context, positions[None, :] < lengths[request],
                            positions[None, :] - context <= step_ids[:, None])
        scores = jnp.where(visible, scores, -jnp.inf)
        row_max = jnp.max(scores, axis=-1, keepdims=True)
        weights = jnp.exp(scores - row_max)
        denominator = jnp.sum(weights, axis=-1)
        heavy = rounded(weights)
        mixed = jnp.einsum('gjst,tgd->sgjd', heavy, value_rows.reshape(-1, HK, HD))
        result = mixed / jnp.transpose(denominator, (2, 0, 1))[..., None]
        return result.reshape(STEPS, HQ * HD).astype(jnp.bfloat16)

    return lax.map(decode_row, jnp.arange(B, dtype=jnp.int32))
```

```python
import jax
import jax.numpy as jnp
from jax import lax
from jax.experimental import pallas as pl
from jax.experimental.pallas import tpu as pltpu
from jax.sharding import PartitionSpec as P

HQ = 64
HK = 8
HD = 128
R = 256
BLOCK = 128
MAXB = 24
STEPS = 4


def project(latent_rows, weight):
    return jnp.dot(latent_rows, weight, preferred_element_type=jnp.float32).astype(jnp.bfloat16)


def attend(key_latent, value_latent, fresh, query, length, up_key, up_value):
    context = key_latent.shape[0]
    key_rows = project(key_latent, up_key)
    value_rows = project(value_latent, up_value)
    group = HQ // HK
    scale = HD ** (-0.5)
    query_heads = query.reshape(STEPS, HK, group, HD)
    fresh_keys = project(fresh[:, :R], up_key).reshape(STEPS, HK, HD)
    fresh_values = project(fresh[:, R:], up_value).reshape(STEPS, HK, HD)
    cached_scores = (
        jnp.einsum(
            "sgjd,tgd->gjst",
            query_heads,
            key_rows.reshape(context, HK, HD),
            preferred_element_type=jnp.float32,
        )
        * scale
    )
    fresh_scores = (
        jnp.einsum("sgjd,tgd->gjst", query_heads, fresh_keys, preferred_element_type=jnp.float32)
        * scale
    )
    cached_mask = jnp.arange(context, dtype=jnp.int32) < length
    step_ids = jnp.arange(STEPS, dtype=jnp.int32)
    fresh_mask = step_ids[None, :] <= step_ids[:, None]
    cached_scores = jnp.where(cached_mask, cached_scores, -jnp.inf)
    fresh_scores = jnp.where(fresh_mask, fresh_scores, -jnp.inf)
    row_max = jnp.maximum(jnp.max(cached_scores, axis=-1), jnp.max(fresh_scores, axis=-1))[
        ..., None
    ]
    cached_weights = jnp.exp(cached_scores - row_max)
    fresh_weights = jnp.exp(fresh_scores - row_max)
    denominator = jnp.sum(cached_weights, axis=-1) + jnp.sum(fresh_weights, axis=-1)
    mixed = jnp.einsum(
        "gjst,tgd->sgjd",
        cached_weights.astype(jnp.bfloat16),
        value_rows.reshape(context, HK, HD),
        preferred_element_type=jnp.float32,
    )
    mixed = mixed + jnp.einsum(
        "gjst,tgd->sgjd",
        fresh_weights.astype(jnp.bfloat16),
        fresh_values,
        preferred_element_type=jnp.float32,
    )
    result = mixed / jnp.transpose(denominator, (2, 0, 1))[..., None]
    return result.reshape(STEPS, HQ * HD).astype(jnp.bfloat16)


def move_blocks(latents, queries, new_latents, up_proj, lengths, place, block_src, block_slot):
    seq_devices = lax.axis_size("seq")
    device = lax.axis_index("seq")
    slot_count = latents.shape[0]
    local_count = queries.shape[0]
    request_count = place.shape[0]
    capacity = (slot_count + seq_devices - 1) // seq_devices
    up_weights = lax.all_gather(up_proj, "seq", axis=1, tiled=True)
    block_ids = jnp.arange(MAXB, dtype=jnp.int32)
    block_counts = (lengths + BLOCK - 1) // BLOCK
    is_live = block_ids[None, :] < block_counts[:, None]
    owners = place // local_count
    entry_ids = jnp.arange(request_count * MAXB, dtype=jnp.int32).reshape(request_count, MAXB)
    held_here = is_live & (block_src == device)
    slot_hits = (
        block_slot[:, :, None] == jnp.arange(slot_count, dtype=jnp.int32)[None, None, :]
    ) & held_here[:, :, None]
    slot_entry = jnp.sum(jnp.where(slot_hits, entry_ids[:, :, None] + 1, 0), axis=(0, 1)) - 1
    slot_used = slot_entry >= 0
    target_dev = owners[jnp.maximum(slot_entry, 0) // MAXB]
    earlier = (
        slot_used[None, :]
        & (target_dev[None, :] == target_dev[:, None])
        & (slot_entry[None, :] < slot_entry[:, None])
    )
    lane_rank = jnp.sum(earlier.astype(jnp.int32), axis=1)
    send_row = jnp.where(slot_used, target_dev * capacity + lane_rank, seq_devices * capacity)
    row_hits = send_row[:, None] == jnp.arange(seq_devices * capacity, dtype=jnp.int32)[None, :]
    source_slot = jnp.sum(
        jnp.where(row_hits, jnp.arange(slot_count, dtype=jnp.int32)[:, None], 0), axis=0
    )
    outgoing = jnp.take(latents, source_slot, axis=0)
    local_rows = device * local_count + jnp.arange(local_count, dtype=jnp.int32)
    requests = jnp.sum(
        jnp.where(
            place[None, :] == local_rows[:, None],
            jnp.arange(request_count, dtype=jnp.int32)[None, :],
            0,
        ),
        axis=1,
    )
    sources = block_src[requests].reshape(-1)
    live_local = is_live[requests].reshape(-1)
    entries = entry_ids[requests].reshape(-1)
    earlier_here = (
        live_local[None, :]
        & (sources[None, :] == sources[:, None])
        & (entries[None, :] < entries[:, None])
    )
    pick_rows = jnp.where(
        live_local, sources * capacity + jnp.sum(earlier_here.astype(jnp.int32), axis=1), 0
    )
    context = MAXB * BLOCK
    incoming = lax.all_to_all(outgoing, "seq", split_axis=0, concat_axis=0, tiled=True)
    gathered = jnp.take(incoming, pick_rows, axis=0).reshape(local_count, context, 2 * R)
    key_latent = gathered[:, :, :R]
    value_latent = gathered[:, :, R:]
    local_lengths = lengths[requests]

    def decode_one(items):
        return attend(
            items[0], items[1], items[2], items[3], items[4], up_weights[0], up_weights[1]
        )

    return lax.map(decode_one, (key_latent, value_latent, new_latents, queries, local_lengths))


GROUP = HQ // HK
ROWS = HQ * STEPS
SCALE = HD ** (-0.5)
CHUNK = 4
NEG = float("-inf")


def slot_plan(lengths, place, block_src, block_slot, device, slot_count):
    starts = jnp.arange(MAXB, dtype=jnp.int32) * BLOCK
    visible = jnp.clip(lengths[:, None] - starts[None, :], 0, BLOCK)
    code = place[:, None] * 256 + visible
    hits = (block_slot[:, :, None] == jnp.arange(slot_count, dtype=jnp.int32)) & (
        block_src == device
    )[:, :, None]
    code = jnp.sum(jnp.where(hits, code[:, :, None], 0), axis=(0, 1))
    return code // 256, code % 256


def scores_kernel(row_ref, vis_ref, lat_ref, q_ref, up_ref, s_ref, m_ref):
    step = pl.program_id(0)

    @pl.when(step == 0)
    def _():
        m_ref[...] = jnp.full(m_ref.shape, NEG, jnp.float32)

    lanes = lax.broadcasted_iota(jnp.int32, (ROWS, BLOCK), 1)
    flat = lat_ref[...].reshape(CHUNK * BLOCK, R)
    keys = project(flat, up_ref[...])
    for c in range(CHUNK):
        row = row_ref[step * CHUNK + c]
        vis = vis_ref[step * CHUNK + c]

        @pl.when(vis > 0)
        def _():
            parts = []
            for g in range(HK):
                parts.append(
                    lax.dot_general(
                        q_ref[row, g * 32 : (g + 1) * 32, :],
                        keys[c * BLOCK : (c + 1) * BLOCK, g * HD : (g + 1) * HD],
                        (((1,), (1,)), ((), ())),
                        preferred_element_type=jnp.float32,
                    )
                )
            s = jnp.concatenate(parts, axis=0) * SCALE
            s = jnp.where(lanes < vis, s, NEG)
            s_ref[c] = s
            m = jnp.max(s, axis=1, keepdims=True)
            m_ref[...] = jnp.where(lanes == row, jnp.maximum(m_ref[...], m), m_ref[...])


def mix_kernel(row_ref, vis_ref, lat_ref, s_ref, m_ref, up_ref, o_ref, l_ref):
    step = pl.program_id(0)

    @pl.when(step == 0)
    def _():
        o_ref[...] = jnp.zeros(o_ref.shape, jnp.float32)
        l_ref[...] = jnp.zeros(l_ref.shape, jnp.float32)

    lanes = lax.broadcasted_iota(jnp.int32, (ROWS, BLOCK), 1)
    flat = lat_ref[...].reshape(CHUNK * BLOCK, R)
    vals = project(flat, up_ref[...])
    for c in range(CHUNK):
        row = row_ref[step * CHUNK + c]
        vis = vis_ref[step * CHUNK + c]

        @pl.when(vis > 0)
        def _():
            m = jnp.max(jnp.where(lanes == row, m_ref[...], NEG), axis=1, keepdims=True)
            p = jnp.exp(s_ref[c] - m)
            total = jnp.sum(p, axis=1, keepdims=True)
            l_ref[...] = jnp.where(lanes == row, l_ref[...] + total, l_ref[...])
            p = p.astype(jnp.bfloat16)
            for g in range(HK):
                o_ref[row, g * 32 : (g + 1) * 32, :] += jnp.dot(
                    p[g * 32 : (g + 1) * 32],
                    vals[c * BLOCK : (c + 1) * BLOCK, g * HD : (g + 1) * HD],
                    preferred_element_type=jnp.float32,
                )


def whole(shape):
    return pl.BlockSpec(shape, lambda i, *_: (0,) * len(shape))


def local(latents, queries, new_latents, up_proj, lengths, place, block_src, block_slot):
    slot_count = latents.shape[0]
    count = queries.shape[0]
    requests = place.shape[0]
    if requests > BLOCK or slot_count % CHUNK:
        return move_blocks(
            latents, queries, new_latents, up_proj, lengths, place, block_src, block_slot
        )
    device = lax.axis_index("seq")
    row, vis = slot_plan(lengths, place, block_src, block_slot, device, slot_count)
    heads = queries.reshape(count, STEPS, HK, GROUP, HD).transpose(0, 2, 1, 3, 4)
    heads = heads.reshape(count, ROWS, HD)
    up = lax.all_gather(up_proj, "seq", axis=1, tiled=True)
    q_all = lax.all_gather(heads, "seq", axis=0, tiled=True)
    steps = slot_count // CHUNK
    s, m = pl.pallas_call(
        scores_kernel,
        grid_spec=pltpu.PrefetchScalarGridSpec(
            num_scalar_prefetch=2,
            grid=(steps,),
            in_specs=[
                pl.BlockSpec((CHUNK, BLOCK, R), lambda i, *_: (i, 0, 0)),
                whole((requests, ROWS, HD)),
                pl.BlockSpec((None, R, HK * HD), lambda i, *_: (0, 0, 0)),
            ],
            out_specs=[
                pl.BlockSpec((CHUNK, ROWS, BLOCK), lambda i, *_: (i, 0, 0)),
                whole((ROWS, BLOCK)),
            ],
        ),
        out_shape=[
            jax.ShapeDtypeStruct((slot_count, ROWS, BLOCK), jnp.float32),
            jax.ShapeDtypeStruct((ROWS, BLOCK), jnp.float32),
        ],
        compiler_params=pltpu.CompilerParams(vmem_limit_bytes=48 * 2**20),
    )(row, vis, latents, q_all, up)
    fresh_k = project(new_latents[:, :, :R], up[0]).reshape(count, STEPS, HK, HD)
    fresh_v = project(new_latents[:, :, R:], up[1]).reshape(count, STEPS, HK, HD)
    q_own = heads.reshape(count, HK, STEPS * GROUP, HD)
    fs = jnp.einsum("bgrd,btgd->bgrt", q_own, fresh_k, preferred_element_type=jnp.float32) * SCALE
    ok = jnp.arange(STEPS)[None, :] <= (jnp.arange(STEPS * GROUP) // GROUP)[:, None]
    fs = jnp.where(ok, fs, NEG)
    fm = jnp.max(fs, axis=-1).reshape(count, ROWS)
    first = device * count
    m = m[:, :requests].T
    own = lax.dynamic_slice(m, (first, 0), (count, ROWS))
    m = lax.dynamic_update_slice(m, jnp.maximum(own, fm), (first, 0))
    m = lax.pmax(m, "seq")
    own = lax.dynamic_slice(m, (first, 0), (count, ROWS)).reshape(count, HK, STEPS * GROUP)
    m_cols = jnp.pad(m.T, ((0, 0), (0, BLOCK - requests)))
    o, l = pl.pallas_call(
        mix_kernel,
        grid_spec=pltpu.PrefetchScalarGridSpec(
            num_scalar_prefetch=2,
            grid=(steps,),
            in_specs=[
                pl.BlockSpec((CHUNK, BLOCK, R), lambda i, *_: (i, 0, 1)),
                pl.BlockSpec((CHUNK, ROWS, BLOCK), lambda i, *_: (i, 0, 0)),
                whole((ROWS, BLOCK)),
                pl.BlockSpec((None, R, HK * HD), lambda i, *_: (1, 0, 0)),
            ],
            out_specs=[whole((requests, ROWS, HD)), whole((ROWS, BLOCK))],
        ),
        out_shape=[
            jax.ShapeDtypeStruct((requests, ROWS, HD), jnp.float32),
            jax.ShapeDtypeStruct((ROWS, BLOCK), jnp.float32),
        ],
        compiler_params=pltpu.CompilerParams(vmem_limit_bytes=48 * 2**20),
    )(row, vis, latents, s, m_cols, up)
    o = lax.psum_scatter(o, "seq", scatter_dimension=0, tiled=True)
    l = lax.psum_scatter(l[:, :requests].T, "seq", scatter_dimension=0, tiled=True)
    fw = jnp.exp(fs - own[..., None])
    l = l.reshape(count, HK, STEPS * GROUP) + jnp.sum(fw, axis=-1)
    o = o.reshape(count, HK, STEPS * GROUP, HD) + jnp.einsum(
        "bgrt,btgd->bgrd", fw.astype(jnp.bfloat16), fresh_v, preferred_element_type=jnp.float32
    )
    o = (o / l[..., None]).astype(jnp.bfloat16)
    o = o.reshape(count, HK, STEPS, GROUP, HD).transpose(0, 2, 1, 3, 4)
    return o.reshape(count, STEPS, HQ * HD)


def solution(mesh):
    return jax.shard_map(
        local,
        mesh=mesh,
        in_specs=(
            P(("groups", "seq"), None, None),
            P(("groups", "seq"), None, None),
            P(("groups", "seq"), None, None),
            P(None, "seq", None),
            P("groups"),
            P("groups"),
            P("groups", None),
            P("groups", None),
        ),
        out_specs=P(("groups", "seq"), None, None),
        check_vma=False,
    )
```

```python
import jax
import jax.numpy as jnp
from jax import lax
from jax.experimental import pallas as pl
from jax.experimental.pallas import tpu as pltpu
from jax.sharding import PartitionSpec as P

HQ = 64
HK = 8
HD = 128
R = 256
BLOCK = 128
MAXB = 24
STEPS = 4


def project(latent_rows, weight):
    return jnp.dot(latent_rows, weight, preferred_element_type=jnp.float32).astype(jnp.bfloat16)


def attend(key_latent, value_latent, fresh, query, length, up_key, up_value):
    context = key_latent.shape[0]
    key_rows = project(key_latent, up_key)
    value_rows = project(value_latent, up_value)
    group = HQ // HK
    scale = HD ** (-0.5)
    query_heads = query.reshape(STEPS, HK, group, HD)
    fresh_keys = project(fresh[:, :R], up_key).reshape(STEPS, HK, HD)
    fresh_values = project(fresh[:, R:], up_value).reshape(STEPS, HK, HD)
    cached_scores = (
        jnp.einsum(
            "sgjd,tgd->gjst",
            query_heads,
            key_rows.reshape(context, HK, HD),
            preferred_element_type=jnp.float32,
        )
        * scale
    )
    fresh_scores = (
        jnp.einsum("sgjd,tgd->gjst", query_heads, fresh_keys, preferred_element_type=jnp.float32)
        * scale
    )
    cached_mask = jnp.arange(context, dtype=jnp.int32) < length
    step_ids = jnp.arange(STEPS, dtype=jnp.int32)
    fresh_mask = step_ids[None, :] <= step_ids[:, None]
    cached_scores = jnp.where(cached_mask, cached_scores, -jnp.inf)
    fresh_scores = jnp.where(fresh_mask, fresh_scores, -jnp.inf)
    row_max = jnp.maximum(jnp.max(cached_scores, axis=-1), jnp.max(fresh_scores, axis=-1))[
        ..., None
    ]
    cached_weights = jnp.exp(cached_scores - row_max)
    fresh_weights = jnp.exp(fresh_scores - row_max)
    denominator = jnp.sum(cached_weights, axis=-1) + jnp.sum(fresh_weights, axis=-1)
    mixed = jnp.einsum(
        "gjst,tgd->sgjd",
        cached_weights.astype(jnp.bfloat16),
        value_rows.reshape(context, HK, HD),
        preferred_element_type=jnp.float32,
    )
    mixed = mixed + jnp.einsum(
        "gjst,tgd->sgjd",
        fresh_weights.astype(jnp.bfloat16),
        fresh_values,
        preferred_element_type=jnp.float32,
    )
    result = mixed / jnp.transpose(denominator, (2, 0, 1))[..., None]
    return result.reshape(STEPS, HQ * HD).astype(jnp.bfloat16)


def move_blocks(latents, queries, new_latents, up_proj, lengths, place, block_src, block_slot):
    seq_devices = lax.axis_size("seq")
    device = lax.axis_index("seq")
    slot_count = latents.shape[0]
    local_count = queries.shape[0]
    request_count = place.shape[0]
    capacity = (slot_count + seq_devices - 1) // seq_devices
    up_weights = lax.all_gather(up_proj, "seq", axis=1, tiled=True)
    block_ids = jnp.arange(MAXB, dtype=jnp.int32)
    block_counts = (lengths + BLOCK - 1) // BLOCK
    is_live = block_ids[None, :] < block_counts[:, None]
    owners = place // local_count
    entry_ids = jnp.arange(request_count * MAXB, dtype=jnp.int32).reshape(request_count, MAXB)
    held_here = is_live & (block_src == device)
    slot_hits = (
        block_slot[:, :, None] == jnp.arange(slot_count, dtype=jnp.int32)[None, None, :]
    ) & held_here[:, :, None]
    slot_entry = jnp.sum(jnp.where(slot_hits, entry_ids[:, :, None] + 1, 0), axis=(0, 1)) - 1
    slot_used = slot_entry >= 0
    target_dev = owners[jnp.maximum(slot_entry, 0) // MAXB]
    earlier = (
        slot_used[None, :]
        & (target_dev[None, :] == target_dev[:, None])
        & (slot_entry[None, :] < slot_entry[:, None])
    )
    lane_rank = jnp.sum(earlier.astype(jnp.int32), axis=1)
    send_row = jnp.where(slot_used, target_dev * capacity + lane_rank, seq_devices * capacity)
    row_hits = send_row[:, None] == jnp.arange(seq_devices * capacity, dtype=jnp.int32)[None, :]
    source_slot = jnp.sum(
        jnp.where(row_hits, jnp.arange(slot_count, dtype=jnp.int32)[:, None], 0), axis=0
    )
    outgoing = jnp.take(latents, source_slot, axis=0)
    local_rows = device * local_count + jnp.arange(local_count, dtype=jnp.int32)
    requests = jnp.sum(
        jnp.where(
            place[None, :] == local_rows[:, None],
            jnp.arange(request_count, dtype=jnp.int32)[None, :],
            0,
        ),
        axis=1,
    )
    sources = block_src[requests].reshape(-1)
    live_local = is_live[requests].reshape(-1)
    entries = entry_ids[requests].reshape(-1)
    earlier_here = (
        live_local[None, :]
        & (sources[None, :] == sources[:, None])
        & (entries[None, :] < entries[:, None])
    )
    pick_rows = jnp.where(
        live_local, sources * capacity + jnp.sum(earlier_here.astype(jnp.int32), axis=1), 0
    )
    context = MAXB * BLOCK
    incoming = lax.all_to_all(outgoing, "seq", split_axis=0, concat_axis=0, tiled=True)
    gathered = jnp.take(incoming, pick_rows, axis=0).reshape(local_count, context, 2 * R)
    key_latent = gathered[:, :, :R]
    value_latent = gathered[:, :, R:]
    local_lengths = lengths[requests]

    def decode_one(items):
        return attend(
            items[0], items[1], items[2], items[3], items[4], up_weights[0], up_weights[1]
        )

    return lax.map(decode_one, (key_latent, value_latent, new_latents, queries, local_lengths))


GROUP = HQ // HK
ROWS = HQ * STEPS
SCALE = HD ** (-0.5)
CHUNK = 4
NEG = float("-inf")


def slot_plan(lengths, place, block_src, block_slot, device, slot_count):
    starts = jnp.arange(MAXB, dtype=jnp.int32) * BLOCK
    visible = jnp.clip(lengths[:, None] - starts[None, :], 0, BLOCK)
    code = place[:, None] * 256 + visible
    hits = (block_slot[:, :, None] == jnp.arange(slot_count, dtype=jnp.int32)) & (
        block_src == device
    )[:, :, None]
    code = jnp.sum(jnp.where(hits, code[:, :, None], 0), axis=(0, 1))
    return code // 256, code % 256


def scores_kernel(row_ref, vis_ref, lat_ref, q_ref, up_ref, s_ref, m_ref):
    step = pl.program_id(0)

    @pl.when(step == 0)
    def _():
        m_ref[...] = jnp.full(m_ref.shape, NEG, jnp.float32)

    lanes = lax.broadcasted_iota(jnp.int32, (ROWS, BLOCK), 1)
    flat = lat_ref[...].reshape(CHUNK * BLOCK, R)
    keys = project(flat, up_ref[...])
    for c in range(CHUNK):
        row = row_ref[step * CHUNK + c]
        vis = vis_ref[step * CHUNK + c]

        @pl.when(vis > 0)
        def _():
            parts = []
            for g in range(HK):
                parts.append(
                    lax.dot_general(
                        q_ref[row, g * 32 : (g + 1) * 32, :],
                        keys[c * BLOCK : (c + 1) * BLOCK, g * HD : (g + 1) * HD],
                        (((1,), (1,)), ((), ())),
                        preferred_element_type=jnp.float32,
                    )
                )
            s = jnp.concatenate(parts, axis=0) * SCALE
            s = jnp.where(lanes < vis, s, NEG)
            s_ref[c] = s
            m = jnp.max(s, axis=1, keepdims=True)
            m_ref[...] = jnp.where(lanes == row, jnp.maximum(m_ref[...], m), m_ref[...])


def mix_kernel(row_ref, vis_ref, lat_ref, s_ref, m_ref, up_ref, out_ref, l_ref, o_ref):
    step = pl.program_id(0)

    @pl.when(step == 0)
    def _():
        o_ref[...] = jnp.zeros(o_ref.shape, jnp.float32)
        l_ref[...] = jnp.zeros(l_ref.shape, jnp.float32)

    lanes = lax.broadcasted_iota(jnp.int32, (ROWS, BLOCK), 1)
    flat = lat_ref[...].reshape(CHUNK * BLOCK, R)
    vals = project(flat, up_ref[...])
    for c in range(CHUNK):
        row = row_ref[step * CHUNK + c]
        vis = vis_ref[step * CHUNK + c]

        @pl.when(vis > 0)
        def _():
            m = jnp.max(jnp.where(lanes == row, m_ref[...], NEG), axis=1, keepdims=True)
            p = jnp.exp(s_ref[c] - m)
            total = jnp.sum(p, axis=1, keepdims=True)
            l_ref[...] = jnp.where(lanes == row, l_ref[...] + total, l_ref[...])
            p = p.astype(jnp.bfloat16)
            for g in range(HK):
                o_ref[row, g * 32 : (g + 1) * 32, :] += jnp.dot(
                    p[g * 32 : (g + 1) * 32],
                    vals[c * BLOCK : (c + 1) * BLOCK, g * HD : (g + 1) * HD],
                    preferred_element_type=jnp.float32,
                )

    @pl.when(step == pl.num_programs(0) - 1)
    def _():
        for r in range(o_ref.shape[0]):
            out_ref[r] = o_ref[r].astype(jnp.bfloat16)


NZ, NY, NC = 4, 2, 2


def coords():
    me = lax.axis_index("seq")
    return me // 4, (me // 2) % 2, me % 2


def at(z, y, c):
    return z * 4 + y * 2 + c


def meet(z, y, c):
    barrier = pltpu.get_barrier_semaphore()
    for d in (at(z, 1 - y, c), at(z, y, 1 - c), *[at((z + k) % NZ, y, c) for k in (1, 2, 3)]):
        pl.semaphore_signal(
            barrier, inc=1, device_id={"seq": d}, device_id_type=pl.DeviceIdType.MESH
        )
    pl.semaphore_wait(barrier, 5)


def send(src, dst, send_sem, recv_sem, dev):
    return pltpu.make_async_remote_copy(
        src_ref=src,
        dst_ref=dst,
        send_sem=send_sem,
        recv_sem=recv_sem,
        device_id={"seq": dev},
        device_id_type=pl.DeviceIdType.MESH,
    )


def gather_kernel(q_ref, up_ref, q_out, up_out, ys, yr, zs, zr, cs, cr, own):
    z, y, c = coords()
    meet(z, y, c)
    depth = up_ref.shape[1]

    def shard(d):
        rows = pl.ds(pl.multiple_of(d * depth, depth), depth)
        return up_out.at[:, rows, :], q_out.at[d]

    def copies(source, d, ssem, rsem, dev):
        return [
            send(s, t, ssem.at[n], rsem.at[n], dev)
            for n, (s, t) in enumerate(zip(source, shard(d)))
        ]

    me = at(z, y, c)
    mine = (up_ref, q_ref)
    local_copies = [
        pltpu.make_async_copy(s, t, own.at[n]) for n, (s, t) in enumerate(zip(mine, shard(me)))
    ]
    y_dev, c_dev = at(z, 1 - y, c), at(z, y, 1 - c)
    y_send, z_send, c_send = [], [], []
    y_send += copies(mine, me, ys.at[0], yr.at[0], y_dev)
    for k in (1, 2, 3):
        z_send += copies(mine, me, zs.at[k], zr.at[k], at((z + k) % NZ, y, c))
    c_send += copies(mine, me, cs.at[0], cr.at[0], c_dev)
    for cp in y_send + z_send + c_send + local_copies:
        cp.start()

    def arrived(d, sem):
        for n, t in enumerate(shard(d)):
            send(t, t, own.at[n], sem.at[n], y_dev).wait_recv()

    def forward(d, ssem, rsem, dev):
        more = copies(shard(d), d, ssem, rsem, dev)
        for cp in more:
            cp.start()
        return more

    arrived(at(z, 1 - y, c), yr.at[0])
    c_send += forward(at(z, 1 - y, c), cs.at[4], cr.at[4], c_dev)
    for k in (1, 2, 3):
        d = at((z - k + NZ) % NZ, y, c)
        arrived(d, zr.at[k])
        y_send += forward(d, ys.at[k], yr.at[k], y_dev)
        c_send += forward(d, cs.at[k], cr.at[k], c_dev)
    for k in (1, 2, 3):
        d = at((z - k + NZ) % NZ, 1 - y, c)
        arrived(d, yr.at[k])
        c_send += forward(d, cs.at[4 + k], cr.at[4 + k], c_dev)
    for k in range(NZ):
        for w in range(NY):
            arrived(at((z - k + NZ) % NZ, (y + w) % NY, 1 - c), cr.at[4 * w + k])
    for cp in y_send + z_send + c_send:
        cp.wait_send()
    for cp in local_copies:
        cp.wait()


def gather(heads, up_proj):
    count, rows, width = heads.shape
    two, depth, cols = up_proj.shape
    n = NZ * NY * NC
    hbm = pl.BlockSpec(memory_space=pl.ANY)
    dma = pltpu.SemaphoreType.DMA
    return pl.pallas_call(
        gather_kernel,
        in_specs=[hbm, hbm],
        out_specs=[hbm, hbm],
        out_shape=[
            jax.ShapeDtypeStruct((n, count, rows, width), heads.dtype),
            jax.ShapeDtypeStruct((two, n * depth, cols), up_proj.dtype),
        ],
        scratch_shapes=[dma((4, 2))] * 4 + [dma((8, 2))] * 2 + [dma((2,))],
        compiler_params=pltpu.CompilerParams(collective_id=0, has_side_effects=True),
    )(heads, up_proj)


def max_kernel(m_ref, out_ref, buf, stage, ss, rs):
    z, y, c = coords()
    meet(z, y, c)
    stage[0] = m_ref[...]
    for n, dev in ((0, at(z, y, 1 - c)), (1, at(z, 1 - y, c))):
        cp = send(stage.at[n], buf.at[n], ss.at[n], rs.at[n], dev)
        cp.start()
        cp.wait()
        stage[n + 1] = jnp.maximum(stage[n], buf[n])
    cps = [
        send(stage.at[2], buf.at[1 + k], ss.at[1 + k], rs.at[1 + k], at((z + k) % NZ, y, c))
        for k in (1, 2, 3)
    ]
    for cp in cps:
        cp.start()
    for cp in cps:
        cp.wait()
    out_ref[...] = jnp.maximum(jnp.maximum(stage[2], buf[2]), jnp.maximum(buf[3], buf[4]))


def global_max(m):
    vmem = pl.BlockSpec(memory_space=pltpu.VMEM)
    dma = pltpu.SemaphoreType.DMA
    return pl.pallas_call(
        max_kernel,
        in_specs=[vmem],
        out_specs=vmem,
        out_shape=jax.ShapeDtypeStruct(m.shape, m.dtype),
        scratch_shapes=[
            pltpu.VMEM((5,) + m.shape, m.dtype),
            pltpu.VMEM((3,) + m.shape, m.dtype),
            dma((5,)),
            dma((5,)),
        ],
        compiler_params=pltpu.CompilerParams(collective_id=1, has_side_effects=True),
    )(m)


def scatter_kernel(o_ref, l_ref, o_out, l_out, cb, cl, yb, yl, yi, yj, zb, zl, zi, zj, cs, cr, ys, yr, zs, zr):
    z, y, c = coords()
    meet(z, y, c)
    y_dev, c_dev = at(z, 1 - y, c), at(z, y, 1 - c)
    order = [(z + 1) % NZ, (z + 2) % NZ, (z + 3) % NZ, z]
    sends = []

    def pair(so, sl, to, tl, ssem, rsem, dev):
        cps = [
            send(so, to, ssem.at[0], rsem.at[0], dev),
            send(sl, tl, ssem.at[1], rsem.at[1], dev),
        ]
        for cp in cps:
            cp.start()
        sends.extend(cps)
        return cps

    c_in = {}
    for w in (1, 0):
        for k in range(NZ):
            d = at(order[k], (y + w) % NY, 1 - c)
            i = 4 * w + k
            c_in[w, k] = pair(
                o_ref.at[d], l_ref.at[d], cb.at[i], cl.at[i], cs.at[i], cr.at[i], c_dev
            )
    f32 = jnp.float32
    y_in = []
    for k in range(NZ):
        for cp in c_in[1, k]:
            cp.wait_recv()
        d = at(order[k], 1 - y, c)
        yb[k] = (o_ref[d].astype(f32) + cb[4 + k].astype(f32)).astype(jnp.bfloat16)
        yl[k] = l_ref[d] + cl[4 + k]
        y_in.append(
            pair(yb.at[k], yl.at[k], yi.at[k], yj.at[k], ys.at[k], yr.at[k], y_dev)
        )
    z_in = []
    for k in range(NZ):
        for cp in c_in[0, k] + y_in[k]:
            cp.wait_recv()
        d = at(order[k], y, c)
        o = o_ref[d].astype(f32) + cb[k].astype(f32) + yi[k].astype(f32)
        l = l_ref[d] + cl[k] + yj[k]
        if k < NZ - 1:
            zb[k] = o.astype(jnp.bfloat16)
            zl[k] = l
            z_in.append(
                pair(
                    zb.at[k], zl.at[k], zi.at[k], zj.at[k], zs.at[k], zr.at[k], at(order[k], y, c)
                )
            )
        else:
            o_out[...] = o
            l_out[...] = l
    for k in range(NZ - 1):
        for cp in z_in[k]:
            cp.wait_recv()
        o_out[...] += zi[k].astype(f32)
        l_out[...] += zj[k]
    for cp in sends:
        cp.wait_send()


def scatter(o, l):
    n, rows, width = o.shape
    lr, lw = l.shape[1:]
    vmem = pl.BlockSpec(memory_space=pltpu.VMEM)
    dma = pltpu.SemaphoreType.DMA

    def bufs(k):
        return [pltpu.VMEM((k, rows, width), o.dtype), pltpu.VMEM((k, lr, lw), l.dtype)]

    return pl.pallas_call(
        scatter_kernel,
        in_specs=[vmem, vmem],
        out_specs=[vmem, vmem],
        out_shape=[
            jax.ShapeDtypeStruct((rows, width), jnp.float32),
            jax.ShapeDtypeStruct((lr, lw), jnp.float32),
        ],
        scratch_shapes=bufs(8) + bufs(4) + bufs(4) + bufs(3) + bufs(3)
        + [dma((8, 2))] * 2 + [dma((4, 2))] * 2 + [dma((3, 2))] * 2,
        compiler_params=pltpu.CompilerParams(
            collective_id=2, has_side_effects=True, vmem_limit_bytes=40 * 2**20
        ),
    )(o, l)


def whole(shape):
    return pl.BlockSpec(shape, lambda i, *_: (0,) * len(shape))


def local(latents, queries, new_latents, up_proj, lengths, place, block_src, block_slot):
    slot_count = latents.shape[0]
    count = queries.shape[0]
    requests = place.shape[0]
    if lax.axis_size("seq") != 16 or requests > BLOCK or slot_count % CHUNK:
        return move_blocks(
            latents, queries, new_latents, up_proj, lengths, place, block_src, block_slot
        )
    device = lax.axis_index("seq")
    row, vis = slot_plan(lengths, place, block_src, block_slot, device, slot_count)
    heads = queries.reshape(count, STEPS, HK, GROUP, HD).transpose(0, 2, 1, 3, 4)
    heads = heads.reshape(count, ROWS, HD)
    q_all, up = gather(heads, up_proj)
    q_all = q_all.reshape(requests, ROWS, HD)
    steps = slot_count // CHUNK
    s, m = pl.pallas_call(
        scores_kernel,
        grid_spec=pltpu.PrefetchScalarGridSpec(
            num_scalar_prefetch=2,
            grid=(steps,),
            in_specs=[
                pl.BlockSpec((CHUNK, BLOCK, R), lambda i, *_: (i, 0, 0)),
                whole((requests, ROWS, HD)),
                pl.BlockSpec((None, R, HK * HD), lambda i, *_: (0, 0, 0)),
            ],
            out_specs=[
                pl.BlockSpec((CHUNK, ROWS, BLOCK), lambda i, *_: (i, 0, 0)),
                whole((ROWS, BLOCK)),
            ],
        ),
        out_shape=[
            jax.ShapeDtypeStruct((slot_count, ROWS, BLOCK), jnp.float32),
            jax.ShapeDtypeStruct((ROWS, BLOCK), jnp.float32),
        ],
        compiler_params=pltpu.CompilerParams(vmem_limit_bytes=48 * 2**20),
    )(row, vis, latents, q_all, up)
    fresh_k = project(new_latents[:, :, :R], up[0]).reshape(count, STEPS, HK, HD)
    fresh_v = project(new_latents[:, :, R:], up[1]).reshape(count, STEPS, HK, HD)
    q_own = heads.reshape(count, HK, STEPS * GROUP, HD)
    fs = jnp.einsum("bgrd,btgd->bgrt", q_own, fresh_k, preferred_element_type=jnp.float32) * SCALE
    ok = jnp.arange(STEPS)[None, :] <= (jnp.arange(STEPS * GROUP) // GROUP)[:, None]
    fs = jnp.where(ok, fs, NEG)
    fm = jnp.max(fs, axis=-1).reshape(count, ROWS)
    first = device * count
    m = m[:, :requests].T
    own = lax.dynamic_slice(m, (first, 0), (count, ROWS))
    m = lax.dynamic_update_slice(m, jnp.maximum(own, fm), (first, 0))
    m = global_max(m)
    own = lax.dynamic_slice(m, (first, 0), (count, ROWS)).reshape(count, HK, STEPS * GROUP)
    m_cols = jnp.pad(m.T, ((0, 0), (0, BLOCK - requests)))
    o, l = pl.pallas_call(
        mix_kernel,
        grid_spec=pltpu.PrefetchScalarGridSpec(
            num_scalar_prefetch=2,
            grid=(steps,),
            in_specs=[
                pl.BlockSpec((CHUNK, BLOCK, R), lambda i, *_: (i, 0, 1)),
                pl.BlockSpec((CHUNK, ROWS, BLOCK), lambda i, *_: (i, 0, 0)),
                whole((ROWS, BLOCK)),
                pl.BlockSpec((None, R, HK * HD), lambda i, *_: (1, 0, 0)),
            ],
            out_specs=[whole((requests, ROWS, HD)), whole((ROWS, BLOCK))],
            scratch_shapes=[pltpu.VMEM((requests, ROWS, HD), jnp.float32)],
        ),
        out_shape=[
            jax.ShapeDtypeStruct((requests, ROWS, HD), jnp.bfloat16),
            jax.ShapeDtypeStruct((ROWS, BLOCK), jnp.float32),
        ],
        compiler_params=pltpu.CompilerParams(vmem_limit_bytes=48 * 2**20),
    )(row, vis, latents, s, m_cols, up)
    devices = lax.axis_size("seq")
    o, l = scatter(
        o.reshape(devices, count * ROWS, HD), l[:, :requests].T.reshape(devices, count, ROWS)
    )
    fw = jnp.exp(fs - own[..., None])
    l = l.reshape(count, HK, STEPS * GROUP) + jnp.sum(fw, axis=-1)
    o = o.reshape(count, HK, STEPS * GROUP, HD) + jnp.einsum(
        "bgrt,btgd->bgrd", fw.astype(jnp.bfloat16), fresh_v, preferred_element_type=jnp.float32
    )
    o = (o / l[..., None]).astype(jnp.bfloat16)
    o = o.reshape(count, HK, STEPS, GROUP, HD).transpose(0, 2, 1, 3, 4)
    return o.reshape(count, STEPS, HQ * HD)


def solution(mesh):
    return jax.shard_map(
        local,
        mesh=mesh,
        in_specs=(
            P(("groups", "seq"), None, None),
            P(("groups", "seq"), None, None),
            P(("groups", "seq"), None, None),
            P(None, "seq", None),
            P("groups"),
            P("groups"),
            P("groups", None),
            P("groups", None),
        ),
        out_specs=P(("groups", "seq"), None, None),
        check_vma=False,
    )
```

```python
import jax
import jax.numpy as jnp
from jax import lax
from jax.experimental import pallas as pl
from jax.experimental.pallas import tpu as pltpu
from jax.sharding import PartitionSpec as P

HQ = 64
HK = 8
HD = 128
R = 256
BLOCK = 128
MAXB = 24
STEPS = 4


def project(latent_rows, weight):
    return jnp.dot(latent_rows, weight, preferred_element_type=jnp.float32).astype(jnp.bfloat16)


def attend(key_latent, value_latent, fresh, query, length, up_key, up_value):
    context = key_latent.shape[0]
    key_rows = project(key_latent, up_key)
    value_rows = project(value_latent, up_value)
    group = HQ // HK
    scale = HD ** (-0.5)
    query_heads = query.reshape(STEPS, HK, group, HD)
    fresh_keys = project(fresh[:, :R], up_key).reshape(STEPS, HK, HD)
    fresh_values = project(fresh[:, R:], up_value).reshape(STEPS, HK, HD)
    cached_scores = (
        jnp.einsum(
            "sgjd,tgd->gjst",
            query_heads,
            key_rows.reshape(context, HK, HD),
            preferred_element_type=jnp.float32,
        )
        * scale
    )
    fresh_scores = (
        jnp.einsum("sgjd,tgd->gjst", query_heads, fresh_keys, preferred_element_type=jnp.float32)
        * scale
    )
    cached_mask = jnp.arange(context, dtype=jnp.int32) < length
    step_ids = jnp.arange(STEPS, dtype=jnp.int32)
    fresh_mask = step_ids[None, :] <= step_ids[:, None]
    cached_scores = jnp.where(cached_mask, cached_scores, -jnp.inf)
    fresh_scores = jnp.where(fresh_mask, fresh_scores, -jnp.inf)
    row_max = jnp.maximum(jnp.max(cached_scores, axis=-1), jnp.max(fresh_scores, axis=-1))[
        ..., None
    ]
    cached_weights = jnp.exp(cached_scores - row_max)
    fresh_weights = jnp.exp(fresh_scores - row_max)
    denominator = jnp.sum(cached_weights, axis=-1) + jnp.sum(fresh_weights, axis=-1)
    mixed = jnp.einsum(
        "gjst,tgd->sgjd",
        cached_weights.astype(jnp.bfloat16),
        value_rows.reshape(context, HK, HD),
        preferred_element_type=jnp.float32,
    )
    mixed = mixed + jnp.einsum(
        "gjst,tgd->sgjd",
        fresh_weights.astype(jnp.bfloat16),
        fresh_values,
        preferred_element_type=jnp.float32,
    )
    result = mixed / jnp.transpose(denominator, (2, 0, 1))[..., None]
    return result.reshape(STEPS, HQ * HD).astype(jnp.bfloat16)


def move_blocks(latents, queries, new_latents, up_proj, lengths, place, block_src, block_slot):
    seq_devices = lax.axis_size("seq")
    device = lax.axis_index("seq")
    slot_count = latents.shape[0]
    local_count = queries.shape[0]
    request_count = place.shape[0]
    capacity = (slot_count + seq_devices - 1) // seq_devices
    up_weights = lax.all_gather(up_proj, "seq", axis=1, tiled=True)
    block_ids = jnp.arange(MAXB, dtype=jnp.int32)
    block_counts = (lengths + BLOCK - 1) // BLOCK
    is_live = block_ids[None, :] < block_counts[:, None]
    owners = place // local_count
    entry_ids = jnp.arange(request_count * MAXB, dtype=jnp.int32).reshape(request_count, MAXB)
    held_here = is_live & (block_src == device)
    slot_hits = (
        block_slot[:, :, None] == jnp.arange(slot_count, dtype=jnp.int32)[None, None, :]
    ) & held_here[:, :, None]
    slot_entry = jnp.sum(jnp.where(slot_hits, entry_ids[:, :, None] + 1, 0), axis=(0, 1)) - 1
    slot_used = slot_entry >= 0
    target_dev = owners[jnp.maximum(slot_entry, 0) // MAXB]
    earlier = (
        slot_used[None, :]
        & (target_dev[None, :] == target_dev[:, None])
        & (slot_entry[None, :] < slot_entry[:, None])
    )
    lane_rank = jnp.sum(earlier.astype(jnp.int32), axis=1)
    send_row = jnp.where(slot_used, target_dev * capacity + lane_rank, seq_devices * capacity)
    row_hits = send_row[:, None] == jnp.arange(seq_devices * capacity, dtype=jnp.int32)[None, :]
    source_slot = jnp.sum(
        jnp.where(row_hits, jnp.arange(slot_count, dtype=jnp.int32)[:, None], 0), axis=0
    )
    outgoing = jnp.take(latents, source_slot, axis=0)
    local_rows = device * local_count + jnp.arange(local_count, dtype=jnp.int32)
    requests = jnp.sum(
        jnp.where(
            place[None, :] == local_rows[:, None],
            jnp.arange(request_count, dtype=jnp.int32)[None, :],
            0,
        ),
        axis=1,
    )
    sources = block_src[requests].reshape(-1)
    live_local = is_live[requests].reshape(-1)
    entries = entry_ids[requests].reshape(-1)
    earlier_here = (
        live_local[None, :]
        & (sources[None, :] == sources[:, None])
        & (entries[None, :] < entries[:, None])
    )
    pick_rows = jnp.where(
        live_local, sources * capacity + jnp.sum(earlier_here.astype(jnp.int32), axis=1), 0
    )
    context = MAXB * BLOCK
    incoming = lax.all_to_all(outgoing, "seq", split_axis=0, concat_axis=0, tiled=True)
    gathered = jnp.take(incoming, pick_rows, axis=0).reshape(local_count, context, 2 * R)
    key_latent = gathered[:, :, :R]
    value_latent = gathered[:, :, R:]
    local_lengths = lengths[requests]

    def decode_one(items):
        return attend(
            items[0], items[1], items[2], items[3], items[4], up_weights[0], up_weights[1]
        )

    return lax.map(decode_one, (key_latent, value_latent, new_latents, queries, local_lengths))


GROUP = HQ // HK
ROWS = HQ * STEPS
SCALE = HD ** (-0.5)
CHUNK = 4
NEG = float("-inf")


def slot_plan(lengths, place, block_src, block_slot, device, slot_count):
    starts = jnp.arange(MAXB, dtype=jnp.int32) * BLOCK
    visible = jnp.clip(lengths[:, None] - starts[None, :], 0, BLOCK)
    code = place[:, None] * 256 + visible
    slots = jnp.arange(slot_count, dtype=jnp.int32)
    hits = (block_slot[:, :, None] == slots) & (block_src == device)[:, :, None]
    code = jnp.sum(jnp.where(hits, code[:, :, None], 0), axis=(0, 1))
    live = code % 256 > 0
    ahead = (live[None, :] & ~live[:, None]) | (
        (live[None, :] == live[:, None]) & (slots[None, :] < slots[:, None])
    )
    rank = jnp.sum(ahead.astype(jnp.int32), axis=1)
    packed = code * 256 + slots
    packed = jnp.sum(jnp.where(rank[:, None] == slots[None, :], packed[:, None], 0), axis=0)
    return packed % 256, packed // 65536, (packed // 256) % 256


def scores_kernel(slot_ref, row_ref, vis_ref, *refs):
    keys = refs[:CHUNK]
    q_ref, s_ref, m_ref = refs[CHUNK:]
    step = pl.program_id(0)

    @pl.when(step == 0)
    def _():
        m_ref[...] = jnp.full(m_ref.shape, NEG, jnp.float32)

    lanes = lax.broadcasted_iota(jnp.int32, (ROWS, BLOCK), 1)

    @pl.when(vis_ref[step * CHUNK] > 0)
    def _():
        best = m_ref[...]
        for c in range(CHUNK):
            row = row_ref[step * CHUNK + c]
            vis = vis_ref[step * CHUNK + c]
            parts = []
            for g in range(HK):
                parts.append(
                    lax.dot_general(
                        q_ref[row, g * 32 : (g + 1) * 32, :],
                        keys[c][:, g * HD : (g + 1) * HD],
                        (((1,), (1,)), ((), ())),
                        preferred_element_type=jnp.float32,
                    )
                )
            s = jnp.concatenate(parts, axis=0) * SCALE
            s = jnp.where(lanes < vis, s, NEG)
            s_ref[c] = s
            m = jnp.max(s, axis=1, keepdims=True)
            best = jnp.where(lanes == row, jnp.maximum(best, m), best)
        m_ref[...] = best


def mix_kernel(slot_ref, row_ref, vis_ref, *refs):
    vals = refs[:CHUNK]
    s_ref, m_ref, out_ref, l_ref, o_ref = refs[CHUNK:]
    step = pl.program_id(0)

    @pl.when(step == 0)
    def _():
        o_ref[...] = jnp.zeros(o_ref.shape, jnp.float32)
        l_ref[...] = jnp.zeros(l_ref.shape, jnp.float32)

    lanes = lax.broadcasted_iota(jnp.int32, (ROWS, BLOCK), 1)

    @pl.when(vis_ref[step * CHUNK] > 0)
    def _():
        best = m_ref[...]
        sums = l_ref[...]
        for c in range(CHUNK):
            row = row_ref[step * CHUNK + c]
            m = jnp.max(jnp.where(lanes == row, best, NEG), axis=1, keepdims=True)
            p = jnp.exp(s_ref[c] - m)
            total = jnp.sum(p, axis=1, keepdims=True)
            sums = jnp.where(lanes == row, sums + total, sums)
            p = p.astype(jnp.bfloat16)
            parts = []
            for g in range(HK):
                parts.append(
                    jnp.dot(
                        p[g * 32 : (g + 1) * 32],
                        vals[c][:, g * HD : (g + 1) * HD],
                        preferred_element_type=jnp.float32,
                    )
                )
            o_ref[row] += jnp.concatenate(parts, axis=0)
        l_ref[...] = sums

    @pl.when(step == pl.num_programs(0) - 1)
    def _():
        for r in range(o_ref.shape[0]):
            out_ref[r] = o_ref[r].astype(jnp.bfloat16)


NZ, NY, NC = 4, 2, 2


def coords():
    me = lax.axis_index("seq")
    return me // 4, (me // 2) % 2, me % 2


def at(z, y, c):
    return z * 4 + y * 2 + c


def meet(z, y, c):
    barrier = pltpu.get_barrier_semaphore()
    for d in (at(z, 1 - y, c), at(z, y, 1 - c), *[at((z + k) % NZ, y, c) for k in (1, 2, 3)]):
        pl.semaphore_signal(
            barrier, inc=1, device_id={"seq": d}, device_id_type=pl.DeviceIdType.MESH
        )
    pl.semaphore_wait(barrier, 5)


def send(src, dst, send_sem, recv_sem, dev):
    return pltpu.make_async_remote_copy(
        src_ref=src,
        dst_ref=dst,
        send_sem=send_sem,
        recv_sem=recv_sem,
        device_id={"seq": dev},
        device_id_type=pl.DeviceIdType.MESH,
    )


def gather_kernel(
    q_ref, up_ref, lat_ref, q_out, up_out, k_out, v_out, ys, yr, zs, zr, cs, cr, own
):
    z, y, c = coords()
    meet(z, y, c)
    depth = up_ref.shape[1]
    me = at(z, y, c)
    y_dev, c_dev = at(z, 1 - y, c), at(z, y, 1 - c)
    sends = []

    def shard(n, d):
        if n == 0:
            return up_out.at[:, pl.ds(pl.multiple_of(d * depth, depth), depth), :]
        return q_out.at[d]

    def post(n, source, d, ssem, rsem, k, dev):
        cp = send(source, shard(n, d), ssem.at[k, n], rsem.at[k, n], dev)
        cp.start()
        sends.append(cp)

    def arrived(n, d, sem, k):
        send(shard(n, d), shard(n, d), own.at[n], sem.at[k, n], y_dev).wait_recv()

    def begin(n):
        mine = (up_ref, q_ref)[n]
        post(n, mine, me, ys, yr, 0, y_dev)
        for k in (1, 2, 3):
            post(n, mine, me, zs, zr, k, at((z + k) % NZ, y, c))
        post(n, mine, me, cs, cr, 0, c_dev)
        cp = pltpu.make_async_copy(mine, shard(n, me), own.at[n])
        cp.start()
        return cp

    def back(k):
        return (z - k + NZ) % NZ

    def from_z(n, k):
        d = at(back(k), y, c)
        arrived(n, d, zr, k)
        post(n, shard(n, d), d, ys, yr, k, y_dev)
        post(n, shard(n, d), d, cs, cr, k, c_dev)

    def from_y(n, k):
        d = at(back(k), 1 - y, c)
        arrived(n, d, yr, k)
        post(n, shard(n, d), d, cs, cr, 4 + k, c_dev)

    def from_c(n):
        for k in range(NZ):
            for w in range(NY):
                arrived(n, at(back(k), (y + w) % NY, 1 - c), cr, 4 * w + k)

    def body(lat, k_blk, v_blk):
        flat = lat[...].reshape(CHUNK * BLOCK, 2 * R)
        k_blk[...] = project(flat[:, :R], up_out[0]).reshape(k_blk.shape)
        v_blk[...] = project(flat[:, R:], up_out[1]).reshape(v_blk.shape)

    def compute(lo, hi):
        def idx(i):
            return (i + lo, 0, 0)

        pltpu.emit_pipeline(
            body,
            grid=(hi - lo,),
            in_specs=[pl.BlockSpec((CHUNK, BLOCK, 2 * R), idx)],
            out_specs=[pl.BlockSpec((CHUNK, BLOCK, HK * HD), idx)] * 2,
        )(lat_ref, k_out, v_out)

    local_copies = [begin(0)]
    local_copies.append(begin(1))
    from_y(0, 0)
    for k in (1, 3, 2):
        from_z(0, k)
    for k in (1, 3, 2):
        from_y(0, k)
    from_c(0)
    local_copies[0].wait()
    steps = lat_ref.shape[0] // CHUNK
    cuts = [0, steps // 4, steps // 2, steps * 3 // 4, steps]
    from_y(1, 0)
    from_z(1, 1)
    compute(cuts[0], cuts[1])
    from_z(1, 3)
    from_z(1, 2)
    compute(cuts[1], cuts[2])
    from_y(1, 1)
    compute(cuts[2], cuts[3])
    from_y(1, 3)
    from_y(1, 2)
    compute(cuts[3], cuts[4])
    from_c(1)
    for cp in sends:
        cp.wait_send()
    local_copies[1].wait()


def gather(heads, up_proj, latents):
    count, rows, width = heads.shape
    two, depth, cols = up_proj.shape
    slots, block = latents.shape[:2]
    n = NZ * NY * NC
    hbm = pl.BlockSpec(memory_space=pl.ANY)
    vmem = pl.BlockSpec(memory_space=pltpu.VMEM)
    dma = pltpu.SemaphoreType.DMA
    return pl.pallas_call(
        gather_kernel,
        in_specs=[hbm, hbm, hbm],
        out_specs=[hbm, vmem, hbm, hbm],
        out_shape=[
            jax.ShapeDtypeStruct((n, count, rows, width), heads.dtype),
            jax.ShapeDtypeStruct((two, n * depth, cols), up_proj.dtype),
            jax.ShapeDtypeStruct((slots, block, cols), up_proj.dtype),
            jax.ShapeDtypeStruct((slots, block, cols), up_proj.dtype),
        ],
        scratch_shapes=[dma((4, 2))] * 4 + [dma((8, 2))] * 2 + [dma((2,))],
        compiler_params=pltpu.CompilerParams(
            collective_id=0, has_side_effects=True, vmem_limit_bytes=40 * 2**20
        ),
    )(heads, up_proj, latents)


def max_kernel(m_ref, out_ref, buf, stage, ss, rs):
    z, y, c = coords()
    meet(z, y, c)
    stage[0] = m_ref[...]
    for n, dev in ((0, at(z, y, 1 - c)), (1, at(z, 1 - y, c))):
        cp = send(stage.at[n], buf.at[n], ss.at[n], rs.at[n], dev)
        cp.start()
        cp.wait()
        stage[n + 1] = jnp.maximum(stage[n], buf[n])
    cps = [
        send(stage.at[2], buf.at[1 + k], ss.at[1 + k], rs.at[1 + k], at((z + k) % NZ, y, c))
        for k in (1, 2, 3)
    ]
    for cp in cps:
        cp.start()
    for cp in cps:
        cp.wait()
    out_ref[...] = jnp.maximum(jnp.maximum(stage[2], buf[2]), jnp.maximum(buf[3], buf[4]))


def global_max(m):
    vmem = pl.BlockSpec(memory_space=pltpu.VMEM)
    dma = pltpu.SemaphoreType.DMA
    return pl.pallas_call(
        max_kernel,
        in_specs=[vmem],
        out_specs=vmem,
        out_shape=jax.ShapeDtypeStruct(m.shape, m.dtype),
        scratch_shapes=[
            pltpu.VMEM((5,) + m.shape, m.dtype),
            pltpu.VMEM((3,) + m.shape, m.dtype),
            dma((5,)),
            dma((5,)),
        ],
        compiler_params=pltpu.CompilerParams(collective_id=1, has_side_effects=True),
    )(m)


def scatter_kernel(o_ref, l_ref, o_out, l_out, cb, cl, yb, yl, yi, yj, zb, zl, zi, zj, cs, cr, ys, yr, zs, zr):
    z, y, c = coords()
    meet(z, y, c)
    y_dev, c_dev = at(z, 1 - y, c), at(z, y, 1 - c)
    order = [(z + 1) % NZ, (z + 2) % NZ, (z + 3) % NZ, z]
    sends = []

    def pair(so, sl, to, tl, ssem, rsem, dev):
        cps = [
            send(so, to, ssem.at[0], rsem.at[0], dev),
            send(sl, tl, ssem.at[1], rsem.at[1], dev),
        ]
        for cp in cps:
            cp.start()
        sends.extend(cps)
        return cps

    c_in = {}
    for w in (1, 0):
        for k in range(NZ):
            d = at(order[k], (y + w) % NY, 1 - c)
            i = 4 * w + k
            c_in[w, k] = pair(
                o_ref.at[d], l_ref.at[d], cb.at[i], cl.at[i], cs.at[i], cr.at[i], c_dev
            )
    f32 = jnp.float32
    y_in = []
    for k in range(NZ):
        for cp in c_in[1, k]:
            cp.wait_recv()
        d = at(order[k], 1 - y, c)
        yb[k] = (o_ref[d].astype(f32) + cb[4 + k].astype(f32)).astype(jnp.bfloat16)
        yl[k] = l_ref[d] + cl[4 + k]
        y_in.append(
            pair(yb.at[k], yl.at[k], yi.at[k], yj.at[k], ys.at[k], yr.at[k], y_dev)
        )
    z_in = []
    for k in range(NZ):
        for cp in c_in[0, k] + y_in[k]:
            cp.wait_recv()
        d = at(order[k], y, c)
        o = o_ref[d].astype(f32) + cb[k].astype(f32) + yi[k].astype(f32)
        l = l_ref[d] + cl[k] + yj[k]
        if k < NZ - 1:
            zb[k] = o.astype(jnp.bfloat16)
            zl[k] = l
            z_in.append(
                pair(
                    zb.at[k], zl.at[k], zi.at[k], zj.at[k], zs.at[k], zr.at[k], at(order[k], y, c)
                )
            )
        else:
            o_out[...] = o
            l_out[...] = l
    for k in range(NZ - 1):
        for cp in z_in[k]:
            cp.wait_recv()
        o_out[...] += zi[k].astype(f32)
        l_out[...] += zj[k]
    for cp in sends:
        cp.wait_send()


def scatter(o, l):
    n, rows, width = o.shape
    lr, lw = l.shape[1:]
    vmem = pl.BlockSpec(memory_space=pltpu.VMEM)
    dma = pltpu.SemaphoreType.DMA

    def bufs(k):
        return [pltpu.VMEM((k, rows, width), o.dtype), pltpu.VMEM((k, lr, lw), l.dtype)]

    return pl.pallas_call(
        scatter_kernel,
        in_specs=[vmem, vmem],
        out_specs=[vmem, vmem],
        out_shape=[
            jax.ShapeDtypeStruct((rows, width), jnp.float32),
            jax.ShapeDtypeStruct((lr, lw), jnp.float32),
        ],
        scratch_shapes=bufs(8) + bufs(4) + bufs(4) + bufs(3) + bufs(3)
        + [dma((8, 2))] * 2 + [dma((4, 2))] * 2 + [dma((3, 2))] * 2,
        compiler_params=pltpu.CompilerParams(
            collective_id=2, has_side_effects=True, vmem_limit_bytes=40 * 2**20
        ),
    )(o, l)


def picked():
    def spec(c):
        return pl.BlockSpec(
            (None, BLOCK, HK * HD), lambda i, slot, row, vis: (slot[i * CHUNK + c], 0, 0)
        )

    return [spec(c) for c in range(CHUNK)]


def whole(shape):
    return pl.BlockSpec(shape, lambda i, *_: (0,) * len(shape))


def local(latents, queries, new_latents, up_proj, lengths, place, block_src, block_slot):
    slot_count = latents.shape[0]
    count = queries.shape[0]
    requests = place.shape[0]
    if lax.axis_size("seq") != 16 or requests > BLOCK or slot_count % CHUNK:
        return move_blocks(
            latents, queries, new_latents, up_proj, lengths, place, block_src, block_slot
        )
    device = lax.axis_index("seq")
    plan = slot_plan(lengths, place, block_src, block_slot, device, slot_count)
    heads = queries.reshape(count, STEPS, HK, GROUP, HD).transpose(0, 2, 1, 3, 4)
    heads = heads.reshape(count, ROWS, HD)
    q_all, up, keys, vals = gather(heads, up_proj, latents)
    q_all = q_all.reshape(requests, ROWS, HD)
    steps = slot_count // CHUNK
    s, m = pl.pallas_call(
        scores_kernel,
        grid_spec=pltpu.PrefetchScalarGridSpec(
            num_scalar_prefetch=3,
            grid=(steps,),
            in_specs=[
                *picked(),
                whole((requests, ROWS, HD)),
            ],
            out_specs=[
                pl.BlockSpec((CHUNK, ROWS, BLOCK), lambda i, *_: (i, 0, 0)),
                whole((ROWS, BLOCK)),
            ],
        ),
        out_shape=[
            jax.ShapeDtypeStruct((slot_count, ROWS, BLOCK), jnp.float32),
            jax.ShapeDtypeStruct((ROWS, BLOCK), jnp.float32),
        ],
        compiler_params=pltpu.CompilerParams(vmem_limit_bytes=48 * 2**20),
    )(*plan, *[keys] * CHUNK, q_all)
    fresh_k = project(new_latents[:, :, :R], up[0]).reshape(count, STEPS, HK, HD)
    fresh_v = project(new_latents[:, :, R:], up[1]).reshape(count, STEPS, HK, HD)
    q_own = heads.reshape(count, HK, STEPS * GROUP, HD)
    fs = jnp.einsum("bgrd,btgd->bgrt", q_own, fresh_k, preferred_element_type=jnp.float32) * SCALE
    ok = jnp.arange(STEPS)[None, :] <= (jnp.arange(STEPS * GROUP) // GROUP)[:, None]
    fs = jnp.where(ok, fs, NEG)
    fm = jnp.max(fs, axis=-1).reshape(count, ROWS)
    first = device * count
    m = m[:, :requests].T
    own = lax.dynamic_slice(m, (first, 0), (count, ROWS))
    m = lax.dynamic_update_slice(m, jnp.maximum(own, fm), (first, 0))
    m = global_max(m)
    own = lax.dynamic_slice(m, (first, 0), (count, ROWS)).reshape(count, HK, STEPS * GROUP)
    m_cols = jnp.pad(m.T, ((0, 0), (0, BLOCK - requests)))
    o, l = pl.pallas_call(
        mix_kernel,
        grid_spec=pltpu.PrefetchScalarGridSpec(
            num_scalar_prefetch=3,
            grid=(steps,),
            in_specs=[
                *picked(),
                pl.BlockSpec((CHUNK, ROWS, BLOCK), lambda i, *_: (i, 0, 0)),
                whole((ROWS, BLOCK)),
            ],
            out_specs=[whole((requests, ROWS, HD)), whole((ROWS, BLOCK))],
            scratch_shapes=[pltpu.VMEM((requests, ROWS, HD), jnp.float32)],
        ),
        out_shape=[
            jax.ShapeDtypeStruct((requests, ROWS, HD), jnp.bfloat16),
            jax.ShapeDtypeStruct((ROWS, BLOCK), jnp.float32),
        ],
        compiler_params=pltpu.CompilerParams(vmem_limit_bytes=48 * 2**20),
    )(*plan, *[vals] * CHUNK, s, m_cols)
    devices = lax.axis_size("seq")
    o, l = scatter(
        o.reshape(devices, count * ROWS, HD), l[:, :requests].T.reshape(devices, count, ROWS)
    )
    fw = jnp.exp(fs - own[..., None])
    l = l.reshape(count, HK, STEPS * GROUP) + jnp.sum(fw, axis=-1)
    o = o.reshape(count, HK, STEPS * GROUP, HD) + jnp.einsum(
        "bgrt,btgd->bgrd", fw.astype(jnp.bfloat16), fresh_v, preferred_element_type=jnp.float32
    )
    o = (o / l[..., None]).astype(jnp.bfloat16)
    o = o.reshape(count, HK, STEPS, GROUP, HD).transpose(0, 2, 1, 3, 4)
    return o.reshape(count, STEPS, HQ * HD)


def solution(mesh):
    return jax.shard_map(
        local,
        mesh=mesh,
        in_specs=(
            P(("groups", "seq"), None, None),
            P(("groups", "seq"), None, None),
            P(("groups", "seq"), None, None),
            P(None, "seq", None),
            P("groups"),
            P("groups"),
            P("groups", None),
            P("groups", None),
        ),
        out_specs=P(("groups", "seq"), None, None),
        check_vma=False,
    )
```

```python
import jax
import jax.numpy as jnp
from jax import lax
from jax.experimental import pallas as pl
from jax.experimental.pallas import tpu as pltpu
from jax.sharding import PartitionSpec as P

HQ = 64
HK = 8
HD = 128
R = 256
BLOCK = 128
MAXB = 24
STEPS = 4


def project(latent_rows, weight):
    return jnp.dot(latent_rows, weight, preferred_element_type=jnp.float32).astype(jnp.bfloat16)


def attend(key_latent, value_latent, fresh, query, length, up_key, up_value):
    context = key_latent.shape[0]
    key_rows = project(key_latent, up_key)
    value_rows = project(value_latent, up_value)
    group = HQ // HK
    scale = HD ** (-0.5)
    query_heads = query.reshape(STEPS, HK, group, HD)
    fresh_keys = project(fresh[:, :R], up_key).reshape(STEPS, HK, HD)
    fresh_values = project(fresh[:, R:], up_value).reshape(STEPS, HK, HD)
    cached_scores = (
        jnp.einsum(
            "sgjd,tgd->gjst",
            query_heads,
            key_rows.reshape(context, HK, HD),
            preferred_element_type=jnp.float32,
        )
        * scale
    )
    fresh_scores = (
        jnp.einsum("sgjd,tgd->gjst", query_heads, fresh_keys, preferred_element_type=jnp.float32)
        * scale
    )
    cached_mask = jnp.arange(context, dtype=jnp.int32) < length
    step_ids = jnp.arange(STEPS, dtype=jnp.int32)
    fresh_mask = step_ids[None, :] <= step_ids[:, None]
    cached_scores = jnp.where(cached_mask, cached_scores, -jnp.inf)
    fresh_scores = jnp.where(fresh_mask, fresh_scores, -jnp.inf)
    row_max = jnp.maximum(jnp.max(cached_scores, axis=-1), jnp.max(fresh_scores, axis=-1))[
        ..., None
    ]
    cached_weights = jnp.exp(cached_scores - row_max)
    fresh_weights = jnp.exp(fresh_scores - row_max)
    denominator = jnp.sum(cached_weights, axis=-1) + jnp.sum(fresh_weights, axis=-1)
    mixed = jnp.einsum(
        "gjst,tgd->sgjd",
        cached_weights.astype(jnp.bfloat16),
        value_rows.reshape(context, HK, HD),
        preferred_element_type=jnp.float32,
    )
    mixed = mixed + jnp.einsum(
        "gjst,tgd->sgjd",
        fresh_weights.astype(jnp.bfloat16),
        fresh_values,
        preferred_element_type=jnp.float32,
    )
    result = mixed / jnp.transpose(denominator, (2, 0, 1))[..., None]
    return result.reshape(STEPS, HQ * HD).astype(jnp.bfloat16)


def move_blocks(latents, queries, new_latents, up_proj, lengths, place, block_src, block_slot):
    seq_devices = lax.axis_size("seq")
    device = lax.axis_index("seq")
    slot_count = latents.shape[0]
    local_count = queries.shape[0]
    request_count = place.shape[0]
    capacity = (slot_count + seq_devices - 1) // seq_devices
    up_weights = lax.all_gather(up_proj, "seq", axis=1, tiled=True)
    block_ids = jnp.arange(MAXB, dtype=jnp.int32)
    block_counts = (lengths + BLOCK - 1) // BLOCK
    is_live = block_ids[None, :] < block_counts[:, None]
    owners = place // local_count
    entry_ids = jnp.arange(request_count * MAXB, dtype=jnp.int32).reshape(request_count, MAXB)
    held_here = is_live & (block_src == device)
    slot_hits = (
        block_slot[:, :, None] == jnp.arange(slot_count, dtype=jnp.int32)[None, None, :]
    ) & held_here[:, :, None]
    slot_entry = jnp.sum(jnp.where(slot_hits, entry_ids[:, :, None] + 1, 0), axis=(0, 1)) - 1
    slot_used = slot_entry >= 0
    target_dev = owners[jnp.maximum(slot_entry, 0) // MAXB]
    earlier = (
        slot_used[None, :]
        & (target_dev[None, :] == target_dev[:, None])
        & (slot_entry[None, :] < slot_entry[:, None])
    )
    lane_rank = jnp.sum(earlier.astype(jnp.int32), axis=1)
    send_row = jnp.where(slot_used, target_dev * capacity + lane_rank, seq_devices * capacity)
    row_hits = send_row[:, None] == jnp.arange(seq_devices * capacity, dtype=jnp.int32)[None, :]
    source_slot = jnp.sum(
        jnp.where(row_hits, jnp.arange(slot_count, dtype=jnp.int32)[:, None], 0), axis=0
    )
    outgoing = jnp.take(latents, source_slot, axis=0)
    local_rows = device * local_count + jnp.arange(local_count, dtype=jnp.int32)
    requests = jnp.sum(
        jnp.where(
            place[None, :] == local_rows[:, None],
            jnp.arange(request_count, dtype=jnp.int32)[None, :],
            0,
        ),
        axis=1,
    )
    sources = block_src[requests].reshape(-1)
    live_local = is_live[requests].reshape(-1)
    entries = entry_ids[requests].reshape(-1)
    earlier_here = (
        live_local[None, :]
        & (sources[None, :] == sources[:, None])
        & (entries[None, :] < entries[:, None])
    )
    pick_rows = jnp.where(
        live_local, sources * capacity + jnp.sum(earlier_here.astype(jnp.int32), axis=1), 0
    )
    context = MAXB * BLOCK
    incoming = lax.all_to_all(outgoing, "seq", split_axis=0, concat_axis=0, tiled=True)
    gathered = jnp.take(incoming, pick_rows, axis=0).reshape(local_count, context, 2 * R)
    key_latent = gathered[:, :, :R]
    value_latent = gathered[:, :, R:]
    local_lengths = lengths[requests]

    def decode_one(items):
        return attend(
            items[0], items[1], items[2], items[3], items[4], up_weights[0], up_weights[1]
        )

    return lax.map(decode_one, (key_latent, value_latent, new_latents, queries, local_lengths))


GROUP = HQ // HK
ROWS = HQ * STEPS
SCALE = HD ** (-0.5)
CHUNK = 4
NEG = float("-inf")


def slot_plan(lengths, place, block_src, block_slot, device, slot_count):
    starts = jnp.arange(MAXB, dtype=jnp.int32) * BLOCK
    visible = jnp.clip(lengths[:, None] - starts[None, :], 0, BLOCK)
    code = place[:, None] * 256 + visible
    slots = jnp.arange(slot_count, dtype=jnp.int32)
    hits = (block_slot[:, :, None] == slots) & (block_src == device)[:, :, None]
    code = jnp.sum(jnp.where(hits, code[:, :, None], 0), axis=(0, 1))
    live = code % 256 > 0
    ahead = (live[None, :] & ~live[:, None]) | (
        (live[None, :] == live[:, None]) & (slots[None, :] < slots[:, None])
    )
    rank = jnp.sum(ahead.astype(jnp.int32), axis=1)
    packed = code * 256 + slots
    packed = jnp.sum(jnp.where(rank[:, None] == slots[None, :], packed[:, None], 0), axis=0)
    return packed % 256, packed // 65536, (packed // 256) % 256


def scores_kernel(slot_ref, row_ref, vis_ref, *refs):
    keys = refs[:CHUNK]
    q_ref, s_ref, m_ref = refs[CHUNK:]
    step = pl.program_id(0)

    @pl.when(step == 0)
    def _():
        m_ref[...] = jnp.full(m_ref.shape, NEG, jnp.float32)

    lanes = lax.broadcasted_iota(jnp.int32, (ROWS, BLOCK), 1)

    @pl.when(vis_ref[step * CHUNK] > 0)
    def _():
        best = m_ref[...]
        for c in range(CHUNK):
            row = row_ref[step * CHUNK + c]
            vis = vis_ref[step * CHUNK + c]
            parts = []
            for g in range(HK):
                parts.append(
                    lax.dot_general(
                        q_ref[row, g * 32 : (g + 1) * 32, :],
                        keys[c][:, g * HD : (g + 1) * HD],
                        (((1,), (1,)), ((), ())),
                        preferred_element_type=jnp.float32,
                    )
                )
            s = jnp.concatenate(parts, axis=0) * SCALE
            s = jnp.where(lanes < vis, s, NEG)
            s_ref[c] = s
            m = jnp.max(s, axis=1, keepdims=True)
            best = jnp.where(lanes == row, jnp.maximum(best, m), best)
        m_ref[...] = best


def mix_kernel(slot_ref, row_ref, vis_ref, *refs):
    vals = refs[:CHUNK]
    s_ref, m_ref, out_ref, l_ref, o_ref = refs[CHUNK:]
    step = pl.program_id(0)

    @pl.when(step == 0)
    def _():
        o_ref[...] = jnp.zeros(o_ref.shape, jnp.float32)
        l_ref[...] = jnp.zeros(l_ref.shape, jnp.float32)

    lanes = lax.broadcasted_iota(jnp.int32, (ROWS, BLOCK), 1)

    @pl.when(vis_ref[step * CHUNK] > 0)
    def _():
        best = m_ref[...]
        sums = l_ref[...]
        for c in range(CHUNK):
            row = row_ref[step * CHUNK + c]
            m = jnp.max(jnp.where(lanes == row, best, NEG), axis=1, keepdims=True)
            p = jnp.exp(s_ref[c] - m)
            total = jnp.sum(p, axis=1, keepdims=True)
            sums = jnp.where(lanes == row, sums + total, sums)
            p = p.astype(jnp.bfloat16)
            parts = []
            for g in range(HK):
                parts.append(
                    jnp.dot(
                        p[g * 32 : (g + 1) * 32],
                        vals[c][:, g * HD : (g + 1) * HD],
                        preferred_element_type=jnp.float32,
                    )
                )
            o_ref[row] += jnp.concatenate(parts, axis=0)
        l_ref[...] = sums

    @pl.when(step == pl.num_programs(0) - 1)
    def _():
        for r in range(o_ref.shape[0]):
            out_ref[r] = o_ref[r].astype(jnp.bfloat16)


NZ, NY, NC = 4, 2, 2


def coords():
    me = lax.axis_index("seq")
    return me // 4, (me // 2) % 2, me % 2


def at(z, y, c):
    return z * 4 + y * 2 + c


def meet(z, y, c):
    barrier = pltpu.get_barrier_semaphore()
    for d in (at(z, 1 - y, c), at(z, y, 1 - c), *[at((z + k) % NZ, y, c) for k in (1, 2, 3)]):
        pl.semaphore_signal(
            barrier, inc=1, device_id={"seq": d}, device_id_type=pl.DeviceIdType.MESH
        )
    pl.semaphore_wait(barrier, 5)


def send(src, dst, send_sem, recv_sem, dev):
    return pltpu.make_async_remote_copy(
        src_ref=src,
        dst_ref=dst,
        send_sem=send_sem,
        recv_sem=recv_sem,
        device_id={"seq": dev},
        device_id_type=pl.DeviceIdType.MESH,
    )


def project_slots(lo, hi, lat_ref, up_ref, out_ref, part):
    def body(lat, out):
        flat = lat[...].reshape(CHUNK * BLOCK, R)
        out[...] = project(flat, up_ref[...]).reshape(out.shape)

    pltpu.emit_pipeline(
        body,
        grid=(hi - lo,),
        in_specs=[pl.BlockSpec((CHUNK, BLOCK, R), lambda i: (i + lo, 0, part))],
        out_specs=[pl.BlockSpec((CHUNK, BLOCK, HK * HD), lambda i: (i + lo, 0, 0))],
    )(lat_ref, out_ref)


def gather_kernel(
    q_ref, up_ref, lat_ref, q_out, up_out, k_out, ys, yr, zs, zr, cs, cr, own
):
    z, y, c = coords()
    meet(z, y, c)
    depth = up_ref.shape[1]
    me = at(z, y, c)
    y_dev, c_dev = at(z, 1 - y, c), at(z, y, 1 - c)
    sends = []

    def shard(n, d):
        if n == 0:
            return up_out.at[:, pl.ds(pl.multiple_of(d * depth, depth), depth), :]
        return q_out.at[d]

    def post(n, source, d, ssem, rsem, k, dev):
        cp = send(source, shard(n, d), ssem.at[k, n], rsem.at[k, n], dev)
        cp.start()
        sends.append(cp)

    def arrived(n, d, sem, k):
        send(shard(n, d), shard(n, d), own.at[n], sem.at[k, n], y_dev).wait_recv()

    def begin(n):
        mine = (up_ref, q_ref)[n]
        post(n, mine, me, ys, yr, 0, y_dev)
        for k in (1, 2, 3):
            post(n, mine, me, zs, zr, k, at((z + k) % NZ, y, c))
        post(n, mine, me, cs, cr, 0, c_dev)
        cp = pltpu.make_async_copy(mine, shard(n, me), own.at[n])
        cp.start()
        return cp

    def back(k):
        return (z - k + NZ) % NZ

    def from_z(n, k):
        d = at(back(k), y, c)
        arrived(n, d, zr, k)
        post(n, shard(n, d), d, ys, yr, k, y_dev)
        post(n, shard(n, d), d, cs, cr, k, c_dev)

    def from_y(n, k):
        d = at(back(k), 1 - y, c)
        arrived(n, d, yr, k)
        post(n, shard(n, d), d, cs, cr, 4 + k, c_dev)

    def from_c(n):
        for k in range(NZ):
            for w in range(NY):
                arrived(n, at(back(k), (y + w) % NY, 1 - c), cr, 4 * w + k)

    def compute(lo, hi):
        project_slots(lo, hi, lat_ref, up_out.at[0], k_out, 0)

    local_copies = [begin(0)]
    local_copies.append(begin(1))
    from_y(0, 0)
    for k in (1, 3, 2):
        from_z(0, k)
    for k in (1, 3, 2):
        from_y(0, k)
    from_c(0)
    local_copies[0].wait()
    steps = lat_ref.shape[0] // CHUNK
    cuts = [0, steps // 4, steps // 2, steps * 3 // 4, steps]
    from_y(1, 0)
    from_z(1, 1)
    compute(cuts[0], cuts[1])
    from_z(1, 3)
    from_z(1, 2)
    compute(cuts[1], cuts[2])
    from_y(1, 1)
    compute(cuts[2], cuts[3])
    from_y(1, 3)
    from_y(1, 2)
    compute(cuts[3], cuts[4])
    from_c(1)
    for cp in sends:
        cp.wait_send()
    local_copies[1].wait()


def gather(heads, up_proj, latents):
    count, rows, width = heads.shape
    two, depth, cols = up_proj.shape
    slots, block = latents.shape[:2]
    n = NZ * NY * NC
    hbm = pl.BlockSpec(memory_space=pl.ANY)
    vmem = pl.BlockSpec(memory_space=pltpu.VMEM)
    dma = pltpu.SemaphoreType.DMA
    return pl.pallas_call(
        gather_kernel,
        in_specs=[hbm, hbm, hbm],
        out_specs=[hbm, vmem, hbm],
        out_shape=[
            jax.ShapeDtypeStruct((n, count, rows, width), heads.dtype),
            jax.ShapeDtypeStruct((two, n * depth, cols), up_proj.dtype),
            jax.ShapeDtypeStruct((slots, block, cols), up_proj.dtype),
        ],
        scratch_shapes=[dma((4, 2))] * 4 + [dma((8, 2))] * 2 + [dma((2,))],
        compiler_params=pltpu.CompilerParams(
            collective_id=0, has_side_effects=True, vmem_limit_bytes=60 * 2**20
        ),
    )(heads, up_proj, latents)


def max_kernel(m_ref, up_ref, lat_ref, out_ref, v_out, buf, stage, ss, rs):
    z, y, c = coords()
    steps = lat_ref.shape[0] // CHUNK
    cuts = [0, steps // 4, steps // 2, steps]
    meet(z, y, c)
    stage[0] = m_ref[...]
    for n, dev in ((0, at(z, y, 1 - c)), (1, at(z, 1 - y, c))):
        cp = send(stage.at[n], buf.at[n], ss.at[n], rs.at[n], dev)
        cp.start()
        project_slots(cuts[n], cuts[n + 1], lat_ref, up_ref.at[1], v_out, 1)
        cp.wait()
        stage[n + 1] = jnp.maximum(stage[n], buf[n])
    cps = [
        send(stage.at[2], buf.at[1 + k], ss.at[1 + k], rs.at[1 + k], at((z + k) % NZ, y, c))
        for k in (1, 2, 3)
    ]
    for cp in cps:
        cp.start()
    project_slots(cuts[2], cuts[3], lat_ref, up_ref.at[1], v_out, 1)
    for cp in cps:
        cp.wait()
    out_ref[...] = jnp.maximum(jnp.maximum(stage[2], buf[2]), jnp.maximum(buf[3], buf[4]))


def global_max(m, up, latents):
    slots, block = latents.shape[:2]
    hbm = pl.BlockSpec(memory_space=pl.ANY)
    vmem = pl.BlockSpec(memory_space=pltpu.VMEM)
    dma = pltpu.SemaphoreType.DMA
    return pl.pallas_call(
        max_kernel,
        in_specs=[vmem, vmem, hbm],
        out_specs=[vmem, hbm],
        out_shape=[
            jax.ShapeDtypeStruct(m.shape, m.dtype),
            jax.ShapeDtypeStruct((slots, block, up.shape[2]), up.dtype),
        ],
        scratch_shapes=[
            pltpu.VMEM((5,) + m.shape, m.dtype),
            pltpu.VMEM((3,) + m.shape, m.dtype),
            dma((5,)),
            dma((5,)),
        ],
        compiler_params=pltpu.CompilerParams(
            collective_id=1, has_side_effects=True, vmem_limit_bytes=60 * 2**20
        ),
    )(m, up, latents)


def scatter_kernel(
    o_ref, l_ref, o_out, l_out, cb, cl, yb, yl, yi, yj, zb, zl, zi, zj, cs, cr, ys, yr, zs, zr
):
    z, y, c = coords()
    meet(z, y, c)
    y_dev, c_dev = at(z, 1 - y, c), at(z, y, 1 - c)
    order = [(z + 1) % NZ, (z + 2) % NZ, (z + 3) % NZ, z]
    half = o_ref.shape[1] // 2
    f32 = jnp.float32
    sends = []

    def rows(h):
        return slice(h * half, (h + 1) * half)

    def piece(h, so, sl, to, tl, ssem, rsem, dev):
        part = pl.ds(h * half, half)
        cps = [send(so.at[part], to.at[part], ssem.at[h], rsem.at[h], dev)]
        if h == 0:
            cps.append(send(sl, tl, ssem.at[2], rsem.at[2], dev))
        for cp in cps:
            cp.start()
        sends.extend(cps)
        return cps

    pieces = [(k, h) for k in range(NZ) for h in (0, 1)]
    c_in, y_in, z_in = {}, {}, {}
    for w in (1, 0):
        for k, h in pieces:
            d = at(order[k], (y + w) % NY, 1 - c)
            i = 4 * w + k
            c_in[w, k, h] = piece(
                h, o_ref.at[d], l_ref.at[d], cb.at[i], cl.at[i], cs.at[i], cr.at[i], c_dev
            )
    for k, h in pieces:
        for cp in c_in[1, k, h]:
            cp.wait_recv()
        d = at(order[k], 1 - y, c)
        yb[k, rows(h)] = (
            o_ref[d, rows(h)].astype(f32) + cb[4 + k, rows(h)].astype(f32)
        ).astype(jnp.bfloat16)
        if h == 0:
            yl[k] = l_ref[d] + cl[4 + k]
        y_in[k, h] = piece(h, yb.at[k], yl.at[k], yi.at[k], yj.at[k], ys.at[k], yr.at[k], y_dev)
    for k, h in pieces:
        for cp in c_in[0, k, h] + y_in[k, h]:
            cp.wait_recv()
        d = at(order[k], y, c)
        o = (
            o_ref[d, rows(h)].astype(f32)
            + cb[k, rows(h)].astype(f32)
            + yi[k, rows(h)].astype(f32)
        )
        if k < NZ - 1:
            zb[k, rows(h)] = o.astype(jnp.bfloat16)
            if h == 0:
                zl[k] = l_ref[d] + cl[k] + yj[k]
            z_in[k, h] = piece(
                h, zb.at[k], zl.at[k], zi.at[k], zj.at[k], zs.at[k], zr.at[k], at(order[k], y, c)
            )
        else:
            o_out[rows(h)] = o
            if h == 0:
                l_out[...] = l_ref[d] + cl[k] + yj[k]
    for k, h in pieces[: 2 * (NZ - 1)]:
        for cp in z_in[k, h]:
            cp.wait_recv()
        o_out[rows(h)] += zi[k, rows(h)].astype(f32)
        if h == 0:
            l_out[...] += zj[k]
    for cp in sends:
        cp.wait_send()


def scatter(o, l):
    n, rows, width = o.shape
    lr, lw = l.shape[1:]
    vmem = pl.BlockSpec(memory_space=pltpu.VMEM)
    dma = pltpu.SemaphoreType.DMA

    def bufs(k):
        return [pltpu.VMEM((k, rows, width), o.dtype), pltpu.VMEM((k, lr, lw), l.dtype)]

    return pl.pallas_call(
        scatter_kernel,
        in_specs=[vmem, vmem],
        out_specs=[vmem, vmem],
        out_shape=[
            jax.ShapeDtypeStruct((rows, width), jnp.float32),
            jax.ShapeDtypeStruct((lr, lw), jnp.float32),
        ],
        scratch_shapes=bufs(8) + bufs(4) + bufs(4) + bufs(3) + bufs(3)
        + [dma((8, 3))] * 2 + [dma((4, 3))] * 2 + [dma((3, 3))] * 2,
        compiler_params=pltpu.CompilerParams(
            collective_id=2, has_side_effects=True, vmem_limit_bytes=40 * 2**20
        ),
    )(o, l)


def picked():
    def spec(c):
        return pl.BlockSpec(
            (None, BLOCK, HK * HD), lambda i, slot, row, vis: (slot[i * CHUNK + c], 0, 0)
        )

    return [spec(c) for c in range(CHUNK)]


def whole(shape):
    return pl.BlockSpec(shape, lambda i, *_: (0,) * len(shape))


def local(latents, queries, new_latents, up_proj, lengths, place, block_src, block_slot):
    slot_count = latents.shape[0]
    count = queries.shape[0]
    requests = place.shape[0]
    if lax.axis_size("seq") != 16 or requests > BLOCK or slot_count % CHUNK:
        return move_blocks(
            latents, queries, new_latents, up_proj, lengths, place, block_src, block_slot
        )
    device = lax.axis_index("seq")
    plan = slot_plan(lengths, place, block_src, block_slot, device, slot_count)
    heads = queries.reshape(count, STEPS, HK, GROUP, HD).transpose(0, 2, 1, 3, 4)
    heads = heads.reshape(count, ROWS, HD)
    q_all, up, keys = gather(heads, up_proj, latents)
    q_all = q_all.reshape(requests, ROWS, HD)
    steps = slot_count // CHUNK
    s, m = pl.pallas_call(
        scores_kernel,
        grid_spec=pltpu.PrefetchScalarGridSpec(
            num_scalar_prefetch=3,
            grid=(steps,),
            in_specs=[
                *picked(),
                whole((requests, ROWS, HD)),
            ],
            out_specs=[
                pl.BlockSpec((CHUNK, ROWS, BLOCK), lambda i, *_: (i, 0, 0)),
                whole((ROWS, BLOCK)),
            ],
        ),
        out_shape=[
            jax.ShapeDtypeStruct((slot_count, ROWS, BLOCK), jnp.float32),
            jax.ShapeDtypeStruct((ROWS, BLOCK), jnp.float32),
        ],
        compiler_params=pltpu.CompilerParams(vmem_limit_bytes=48 * 2**20),
    )(*plan, *[keys] * CHUNK, q_all)
    fresh_k = project(new_latents[:, :, :R], up[0]).reshape(count, STEPS, HK, HD)
    fresh_v = project(new_latents[:, :, R:], up[1]).reshape(count, STEPS, HK, HD)
    q_own = heads.reshape(count, HK, STEPS * GROUP, HD)
    fs = jnp.einsum("bgrd,btgd->bgrt", q_own, fresh_k, preferred_element_type=jnp.float32) * SCALE
    ok = jnp.arange(STEPS)[None, :] <= (jnp.arange(STEPS * GROUP) // GROUP)[:, None]
    fs = jnp.where(ok, fs, NEG)
    fm = jnp.max(fs, axis=-1).reshape(count, ROWS)
    first = device * count
    m = m[:, :requests].T
    own = lax.dynamic_slice(m, (first, 0), (count, ROWS))
    m = lax.dynamic_update_slice(m, jnp.maximum(own, fm), (first, 0))
    m, vals = global_max(m, up, latents)
    own = lax.dynamic_slice(m, (first, 0), (count, ROWS)).reshape(count, HK, STEPS * GROUP)
    m_cols = jnp.pad(m.T, ((0, 0), (0, BLOCK - requests)))
    o, l = pl.pallas_call(
        mix_kernel,
        grid_spec=pltpu.PrefetchScalarGridSpec(
            num_scalar_prefetch=3,
            grid=(steps,),
            in_specs=[
                *picked(),
                pl.BlockSpec((CHUNK, ROWS, BLOCK), lambda i, *_: (i, 0, 0)),
                whole((ROWS, BLOCK)),
            ],
            out_specs=[whole((requests, ROWS, HD)), whole((ROWS, BLOCK))],
            scratch_shapes=[pltpu.VMEM((requests, ROWS, HD), jnp.float32)],
        ),
        out_shape=[
            jax.ShapeDtypeStruct((requests, ROWS, HD), jnp.bfloat16),
            jax.ShapeDtypeStruct((ROWS, BLOCK), jnp.float32),
        ],
        compiler_params=pltpu.CompilerParams(vmem_limit_bytes=48 * 2**20),
    )(*plan, *[vals] * CHUNK, s, m_cols)
    devices = lax.axis_size("seq")
    o, l = scatter(
        o.reshape(devices, count * ROWS, HD), l[:, :requests].T.reshape(devices, count, ROWS)
    )
    fw = jnp.exp(fs - own[..., None])
    l = l.reshape(count, HK, STEPS * GROUP) + jnp.sum(fw, axis=-1)
    o = o.reshape(count, HK, STEPS * GROUP, HD) + jnp.einsum(
        "bgrt,btgd->bgrd", fw.astype(jnp.bfloat16), fresh_v, preferred_element_type=jnp.float32
    )
    o = (o / l[..., None]).astype(jnp.bfloat16)
    o = o.reshape(count, HK, STEPS, GROUP, HD).transpose(0, 2, 1, 3, 4)
    return o.reshape(count, STEPS, HQ * HD)


def solution(mesh):
    return jax.shard_map(
        local,
        mesh=mesh,
        in_specs=(
            P(("groups", "seq"), None, None),
            P(("groups", "seq"), None, None),
            P(("groups", "seq"), None, None),
            P(None, "seq", None),
            P("groups"),
            P("groups"),
            P("groups", None),
            P("groups", None),
        ),
        out_specs=P(("groups", "seq"), None, None),
        check_vma=False,
    )
```

```python
import jax
import jax.numpy as jnp
from jax import lax
from jax.experimental import pallas as pl
from jax.experimental.pallas import tpu as pltpu
from jax.sharding import PartitionSpec as P

HQ = 64
HK = 8
HD = 128
R = 256
BLOCK = 128
MAXB = 24
STEPS = 4


def project(latent_rows, weight):
    return jnp.dot(latent_rows, weight, preferred_element_type=jnp.float32).astype(jnp.bfloat16)


def attend(key_latent, value_latent, fresh, query, length, up_key, up_value):
    context = key_latent.shape[0]
    key_rows = project(key_latent, up_key)
    value_rows = project(value_latent, up_value)
    group = HQ // HK
    scale = HD ** (-0.5)
    query_heads = query.reshape(STEPS, HK, group, HD)
    fresh_keys = project(fresh[:, :R], up_key).reshape(STEPS, HK, HD)
    fresh_values = project(fresh[:, R:], up_value).reshape(STEPS, HK, HD)
    cached_scores = (
        jnp.einsum(
            "sgjd,tgd->gjst",
            query_heads,
            key_rows.reshape(context, HK, HD),
            preferred_element_type=jnp.float32,
        )
        * scale
    )
    fresh_scores = (
        jnp.einsum("sgjd,tgd->gjst", query_heads, fresh_keys, preferred_element_type=jnp.float32)
        * scale
    )
    cached_mask = jnp.arange(context, dtype=jnp.int32) < length
    step_ids = jnp.arange(STEPS, dtype=jnp.int32)
    fresh_mask = step_ids[None, :] <= step_ids[:, None]
    cached_scores = jnp.where(cached_mask, cached_scores, -jnp.inf)
    fresh_scores = jnp.where(fresh_mask, fresh_scores, -jnp.inf)
    row_max = jnp.maximum(jnp.max(cached_scores, axis=-1), jnp.max(fresh_scores, axis=-1))[
        ..., None
    ]
    cached_weights = jnp.exp(cached_scores - row_max)
    fresh_weights = jnp.exp(fresh_scores - row_max)
    denominator = jnp.sum(cached_weights, axis=-1) + jnp.sum(fresh_weights, axis=-1)
    mixed = jnp.einsum(
        "gjst,tgd->sgjd",
        cached_weights.astype(jnp.bfloat16),
        value_rows.reshape(context, HK, HD),
        preferred_element_type=jnp.float32,
    )
    mixed = mixed + jnp.einsum(
        "gjst,tgd->sgjd",
        fresh_weights.astype(jnp.bfloat16),
        fresh_values,
        preferred_element_type=jnp.float32,
    )
    result = mixed / jnp.transpose(denominator, (2, 0, 1))[..., None]
    return result.reshape(STEPS, HQ * HD).astype(jnp.bfloat16)


def move_blocks(latents, queries, new_latents, up_proj, lengths, place, block_src, block_slot):
    seq_devices = lax.axis_size("seq")
    device = lax.axis_index("seq")
    slot_count = latents.shape[0]
    local_count = queries.shape[0]
    request_count = place.shape[0]
    capacity = (slot_count + seq_devices - 1) // seq_devices
    up_weights = lax.all_gather(up_proj, "seq", axis=1, tiled=True)
    block_ids = jnp.arange(MAXB, dtype=jnp.int32)
    block_counts = (lengths + BLOCK - 1) // BLOCK
    is_live = block_ids[None, :] < block_counts[:, None]
    owners = place // local_count
    entry_ids = jnp.arange(request_count * MAXB, dtype=jnp.int32).reshape(request_count, MAXB)
    held_here = is_live & (block_src == device)
    slot_hits = (
        block_slot[:, :, None] == jnp.arange(slot_count, dtype=jnp.int32)[None, None, :]
    ) & held_here[:, :, None]
    slot_entry = jnp.sum(jnp.where(slot_hits, entry_ids[:, :, None] + 1, 0), axis=(0, 1)) - 1
    slot_used = slot_entry >= 0
    target_dev = owners[jnp.maximum(slot_entry, 0) // MAXB]
    earlier = (
        slot_used[None, :]
        & (target_dev[None, :] == target_dev[:, None])
        & (slot_entry[None, :] < slot_entry[:, None])
    )
    lane_rank = jnp.sum(earlier.astype(jnp.int32), axis=1)
    send_row = jnp.where(slot_used, target_dev * capacity + lane_rank, seq_devices * capacity)
    row_hits = send_row[:, None] == jnp.arange(seq_devices * capacity, dtype=jnp.int32)[None, :]
    source_slot = jnp.sum(
        jnp.where(row_hits, jnp.arange(slot_count, dtype=jnp.int32)[:, None], 0), axis=0
    )
    outgoing = jnp.take(latents, source_slot, axis=0)
    local_rows = device * local_count + jnp.arange(local_count, dtype=jnp.int32)
    requests = jnp.sum(
        jnp.where(
            place[None, :] == local_rows[:, None],
            jnp.arange(request_count, dtype=jnp.int32)[None, :],
            0,
        ),
        axis=1,
    )
    sources = block_src[requests].reshape(-1)
    live_local = is_live[requests].reshape(-1)
    entries = entry_ids[requests].reshape(-1)
    earlier_here = (
        live_local[None, :]
        & (sources[None, :] == sources[:, None])
        & (entries[None, :] < entries[:, None])
    )
    pick_rows = jnp.where(
        live_local, sources * capacity + jnp.sum(earlier_here.astype(jnp.int32), axis=1), 0
    )
    context = MAXB * BLOCK
    incoming = lax.all_to_all(outgoing, "seq", split_axis=0, concat_axis=0, tiled=True)
    gathered = jnp.take(incoming, pick_rows, axis=0).reshape(local_count, context, 2 * R)
    key_latent = gathered[:, :, :R]
    value_latent = gathered[:, :, R:]
    local_lengths = lengths[requests]

    def decode_one(items):
        return attend(
            items[0], items[1], items[2], items[3], items[4], up_weights[0], up_weights[1]
        )

    return lax.map(decode_one, (key_latent, value_latent, new_latents, queries, local_lengths))


GROUP = HQ // HK
ROWS = HQ * STEPS
SCALE = HD ** (-0.5)
CHUNK = 4
NEG = float("-inf")


def slot_plan(lengths, place, block_src, block_slot, device, slot_count):
    starts = jnp.arange(MAXB, dtype=jnp.int32) * BLOCK
    visible = jnp.clip(lengths[:, None] - starts[None, :], 0, BLOCK)
    code = place[:, None] * 256 + visible
    slots = jnp.arange(slot_count, dtype=jnp.int32)
    hits = (block_slot[:, :, None] == slots) & (block_src == device)[:, :, None]
    code = jnp.sum(jnp.where(hits, code[:, :, None], 0), axis=(0, 1))
    live = code % 256 > 0
    ahead = (live[None, :] & ~live[:, None]) | (
        (live[None, :] == live[:, None]) & (slots[None, :] < slots[:, None])
    )
    rank = jnp.sum(ahead.astype(jnp.int32), axis=1)
    packed = code * 256 + slots
    packed = jnp.sum(jnp.where(rank[:, None] == slots[None, :], packed[:, None], 0), axis=0)
    return packed % 256, packed // 65536, (packed // 256) % 256


def scores_kernel(slot_ref, row_ref, vis_ref, *refs):
    keys = refs[:CHUNK]
    q_ref, s_ref, m_ref = refs[CHUNK:]
    step = pl.program_id(0)

    @pl.when(step == 0)
    def _():
        m_ref[...] = jnp.full(m_ref.shape, NEG, jnp.float32)

    lanes = lax.broadcasted_iota(jnp.int32, (ROWS, BLOCK), 1)

    @pl.when(vis_ref[step * CHUNK] > 0)
    def _():
        best = m_ref[...]
        for c in range(CHUNK):
            row = row_ref[step * CHUNK + c]
            vis = vis_ref[step * CHUNK + c]
            parts = []
            for g in range(HK):
                parts.append(
                    lax.dot_general(
                        q_ref[row, g * 32 : (g + 1) * 32, :],
                        keys[c][:, g * HD : (g + 1) * HD],
                        (((1,), (1,)), ((), ())),
                        preferred_element_type=jnp.float32,
                    )
                )
            s = jnp.concatenate(parts, axis=0) * SCALE
            s = jnp.where(lanes < vis, s, NEG)
            s_ref[c] = s
            m = jnp.max(s, axis=1, keepdims=True)
            best = jnp.where(lanes == row, jnp.maximum(best, m), best)
        m_ref[...] = best


def mix_kernel(slot_ref, row_ref, vis_ref, *refs):
    vals = refs[:CHUNK]
    s_ref, m_ref, out_ref, l_ref, o_ref = refs[CHUNK:]
    step = pl.program_id(0)

    @pl.when(step == 0)
    def _():
        o_ref[...] = jnp.zeros(o_ref.shape, jnp.float32)
        l_ref[...] = jnp.zeros(l_ref.shape, jnp.float32)

    lanes = lax.broadcasted_iota(jnp.int32, (ROWS, BLOCK), 1)

    @pl.when(vis_ref[step * CHUNK] > 0)
    def _():
        best = m_ref[...]
        sums = l_ref[...]
        for c in range(CHUNK):
            row = row_ref[step * CHUNK + c]
            m = jnp.max(jnp.where(lanes == row, best, NEG), axis=1, keepdims=True)
            p = jnp.exp(s_ref[c] - m)
            total = jnp.sum(p, axis=1, keepdims=True)
            sums = jnp.where(lanes == row, sums + total, sums)
            p = p.astype(jnp.bfloat16)
            parts = []
            for g in range(HK):
                parts.append(
                    jnp.dot(
                        p[g * 32 : (g + 1) * 32],
                        vals[c][:, g * HD : (g + 1) * HD],
                        preferred_element_type=jnp.float32,
                    )
                )
            o_ref[row] += jnp.concatenate(parts, axis=0)
        l_ref[...] = sums

    @pl.when(step == pl.num_programs(0) - 1)
    def _():
        for r in range(o_ref.shape[0]):
            out_ref[r] = o_ref[r].astype(jnp.bfloat16)


NZ, NY, NC = 4, 2, 2


def coords():
    me = lax.axis_index("seq")
    return me // 4, (me // 2) % 2, me % 2


def at(z, y, c):
    return z * 4 + y * 2 + c


def meet(z, y, c):
    barrier = pltpu.get_barrier_semaphore()
    for d in (at(z, 1 - y, c), at(z, y, 1 - c), *[at((z + k) % NZ, y, c) for k in (1, 2, 3)]):
        pl.semaphore_signal(
            barrier, inc=1, device_id={"seq": d}, device_id_type=pl.DeviceIdType.MESH
        )
    pl.semaphore_wait(barrier, 5)


def send(src, dst, send_sem, recv_sem, dev):
    return pltpu.make_async_remote_copy(
        src_ref=src,
        dst_ref=dst,
        send_sem=send_sem,
        recv_sem=recv_sem,
        device_id={"seq": dev},
        device_id_type=pl.DeviceIdType.MESH,
    )


def gather_kernel(
    q_ref, up_ref, lat_ref, q_out, up_out, k_out, v_out, ys, yr, zs, zr, cs, cr, own
):
    z, y, c = coords()
    meet(z, y, c)
    depth = up_ref.shape[1]
    me = at(z, y, c)
    y_dev, c_dev = at(z, 1 - y, c), at(z, y, 1 - c)
    sends = []

    def shard(n, d):
        if n == 0:
            return up_out.at[:, pl.ds(pl.multiple_of(d * depth, depth), depth), :]
        return q_out.at[d]

    def post(n, source, d, ssem, rsem, k, dev):
        cp = send(source, shard(n, d), ssem.at[k, n], rsem.at[k, n], dev)
        cp.start()
        sends.append(cp)

    def arrived(n, d, sem, k):
        send(shard(n, d), shard(n, d), own.at[n], sem.at[k, n], y_dev).wait_recv()

    def begin(n):
        mine = (up_ref, q_ref)[n]
        post(n, mine, me, ys, yr, 0, y_dev)
        for k in (1, 2, 3):
            post(n, mine, me, zs, zr, k, at((z + k) % NZ, y, c))
        post(n, mine, me, cs, cr, 0, c_dev)
        cp = pltpu.make_async_copy(mine, shard(n, me), own.at[n])
        cp.start()
        return cp

    def back(k):
        return (z - k + NZ) % NZ

    def from_z(n, k):
        d = at(back(k), y, c)
        arrived(n, d, zr, k)
        post(n, shard(n, d), d, ys, yr, k, y_dev)
        post(n, shard(n, d), d, cs, cr, k, c_dev)

    def from_y(n, k):
        d = at(back(k), 1 - y, c)
        arrived(n, d, yr, k)
        post(n, shard(n, d), d, cs, cr, 4 + k, c_dev)

    def from_c(n):
        for k in range(NZ):
            for w in range(NY):
                arrived(n, at(back(k), (y + w) % NY, 1 - c), cr, 4 * w + k)

    def body(lat, k_blk, v_blk):
        flat = lat[...].reshape(CHUNK * BLOCK, 2 * R)
        k_blk[...] = project(flat[:, :R], up_out[0]).reshape(k_blk.shape)
        v_blk[...] = project(flat[:, R:], up_out[1]).reshape(v_blk.shape)

    def compute(lo, hi):
        def idx(i):
            return (i + lo, 0, 0)

        pltpu.emit_pipeline(
            body,
            grid=(hi - lo,),
            in_specs=[pl.BlockSpec((CHUNK, BLOCK, 2 * R), idx)],
            out_specs=[pl.BlockSpec((CHUNK, BLOCK, HK * HD), idx)] * 2,
        )(lat_ref, k_out, v_out)

    local_copies = [begin(0)]
    local_copies.append(begin(1))
    from_y(0, 0)
    for k in (1, 3, 2):
        from_z(0, k)
    for k in (1, 3, 2):
        from_y(0, k)
    from_c(0)
    local_copies[0].wait()
    steps = lat_ref.shape[0] // CHUNK
    cuts = [0, steps // 4, steps // 2, steps * 3 // 4, steps]
    from_y(1, 0)
    from_z(1, 1)
    compute(cuts[0], cuts[1])
    from_z(1, 3)
    from_z(1, 2)
    compute(cuts[1], cuts[2])
    from_y(1, 1)
    compute(cuts[2], cuts[3])
    from_y(1, 3)
    from_y(1, 2)
    compute(cuts[3], cuts[4])
    from_c(1)
    for cp in sends:
        cp.wait_send()
    local_copies[1].wait()


def gather(heads, up_proj, latents):
    count, rows, width = heads.shape
    two, depth, cols = up_proj.shape
    slots, block = latents.shape[:2]
    n = NZ * NY * NC
    hbm = pl.BlockSpec(memory_space=pl.ANY)
    vmem = pl.BlockSpec(memory_space=pltpu.VMEM)
    dma = pltpu.SemaphoreType.DMA
    return pl.pallas_call(
        gather_kernel,
        in_specs=[hbm, hbm, hbm],
        out_specs=[hbm, vmem, hbm, hbm],
        out_shape=[
            jax.ShapeDtypeStruct((n, count, rows, width), heads.dtype),
            jax.ShapeDtypeStruct((two, n * depth, cols), up_proj.dtype),
            jax.ShapeDtypeStruct((slots, block, cols), up_proj.dtype),
            jax.ShapeDtypeStruct((slots, block, cols), up_proj.dtype),
        ],
        scratch_shapes=[dma((4, 2))] * 4 + [dma((8, 2))] * 2 + [dma((2,))],
        compiler_params=pltpu.CompilerParams(
            collective_id=0, has_side_effects=True, vmem_limit_bytes=60 * 2**20
        ),
    )(heads, up_proj, latents)


def max_kernel(m_ref, out_ref, buf, stage, ss, rs):
    z, y, c = coords()
    meet(z, y, c)
    stage[0] = m_ref[...]
    for n, dev in ((0, at(z, y, 1 - c)), (1, at(z, 1 - y, c))):
        cp = send(stage.at[n], buf.at[n], ss.at[n], rs.at[n], dev)
        cp.start()
        cp.wait()
        stage[n + 1] = jnp.maximum(stage[n], buf[n])
    cps = [
        send(stage.at[2], buf.at[1 + k], ss.at[1 + k], rs.at[1 + k], at((z + k) % NZ, y, c))
        for k in (1, 2, 3)
    ]
    for cp in cps:
        cp.start()
    for cp in cps:
        cp.wait()
    out_ref[...] = jnp.maximum(jnp.maximum(stage[2], buf[2]), jnp.maximum(buf[3], buf[4]))


def global_max(m):
    vmem = pl.BlockSpec(memory_space=pltpu.VMEM)
    dma = pltpu.SemaphoreType.DMA
    return pl.pallas_call(
        max_kernel,
        in_specs=[vmem],
        out_specs=vmem,
        out_shape=jax.ShapeDtypeStruct(m.shape, m.dtype),
        scratch_shapes=[
            pltpu.VMEM((5,) + m.shape, m.dtype),
            pltpu.VMEM((3,) + m.shape, m.dtype),
            dma((5,)),
            dma((5,)),
        ],
        compiler_params=pltpu.CompilerParams(collective_id=1, has_side_effects=True),
    )(m)


def scatter_kernel(
    o_ref, l_ref, o_out, l_out, cb, cl, yb, yl, yi, yj, zb, zl, zi, zj, cs, cr, ys, yr, zs, zr
):
    z, y, c = coords()
    meet(z, y, c)
    y_dev, c_dev = at(z, 1 - y, c), at(z, y, 1 - c)
    order = [(z + 1) % NZ, (z + 2) % NZ, (z + 3) % NZ, z]
    half = o_ref.shape[1] // 2
    f32 = jnp.float32
    sends = []

    def rows(h):
        return slice(h * half, (h + 1) * half)

    def piece(h, so, sl, to, tl, ssem, rsem, dev):
        part = pl.ds(h * half, half)
        cps = [send(so.at[part], to.at[part], ssem.at[h], rsem.at[h], dev)]
        if h == 0:
            cps.append(send(sl, tl, ssem.at[2], rsem.at[2], dev))
        for cp in cps:
            cp.start()
        sends.extend(cps)
        return cps

    pieces = [(k, h) for k in range(NZ) for h in (0, 1)]
    c_in, y_in, z_in = {}, {}, {}
    for w in (1, 0):
        for k, h in pieces:
            d = at(order[k], (y + w) % NY, 1 - c)
            i = 4 * w + k
            c_in[w, k, h] = piece(
                h, o_ref.at[d], l_ref.at[d], cb.at[i], cl.at[i], cs.at[i], cr.at[i], c_dev
            )
    for k, h in pieces:
        for cp in c_in[1, k, h]:
            cp.wait_recv()
        d = at(order[k], 1 - y, c)
        yb[k, rows(h)] = (
            o_ref[d, rows(h)].astype(f32) + cb[4 + k, rows(h)].astype(f32)
        ).astype(jnp.bfloat16)
        if h == 0:
            yl[k] = l_ref[d] + cl[4 + k]
        y_in[k, h] = piece(h, yb.at[k], yl.at[k], yi.at[k], yj.at[k], ys.at[k], yr.at[k], y_dev)
    for k, h in pieces:
        for cp in c_in[0, k, h] + y_in[k, h]:
            cp.wait_recv()
        d = at(order[k], y, c)
        o = (
            o_ref[d, rows(h)].astype(f32)
            + cb[k, rows(h)].astype(f32)
            + yi[k, rows(h)].astype(f32)
        )
        if k < NZ - 1:
            zb[k, rows(h)] = o.astype(jnp.bfloat16)
            if h == 0:
                zl[k] = l_ref[d] + cl[k] + yj[k]
            z_in[k, h] = piece(
                h, zb.at[k], zl.at[k], zi.at[k], zj.at[k], zs.at[k], zr.at[k], at(order[k], y, c)
            )
        else:
            o_out[rows(h)] = o
            if h == 0:
                l_out[...] = l_ref[d] + cl[k] + yj[k]
    for k, h in pieces[: 2 * (NZ - 1)]:
        for cp in z_in[k, h]:
            cp.wait_recv()
        o_out[rows(h)] += zi[k, rows(h)].astype(f32)
        if h == 0:
            l_out[...] += zj[k]
    for cp in sends:
        cp.wait_send()


def scatter(o, l):
    n, rows, width = o.shape
    lr, lw = l.shape[1:]
    vmem = pl.BlockSpec(memory_space=pltpu.VMEM)
    dma = pltpu.SemaphoreType.DMA

    def bufs(k):
        return [pltpu.VMEM((k, rows, width), o.dtype), pltpu.VMEM((k, lr, lw), l.dtype)]

    return pl.pallas_call(
        scatter_kernel,
        in_specs=[vmem, vmem],
        out_specs=[vmem, vmem],
        out_shape=[
            jax.ShapeDtypeStruct((rows, width), jnp.float32),
            jax.ShapeDtypeStruct((lr, lw), jnp.float32),
        ],
        scratch_shapes=bufs(8) + bufs(4) + bufs(4) + bufs(3) + bufs(3)
        + [dma((8, 3))] * 2 + [dma((4, 3))] * 2 + [dma((3, 3))] * 2,
        compiler_params=pltpu.CompilerParams(
            collective_id=2, has_side_effects=True, vmem_limit_bytes=40 * 2**20
        ),
    )(o, l)


def picked():
    def spec(c):
        return pl.BlockSpec(
            (None, BLOCK, HK * HD), lambda i, slot, row, vis: (slot[i * CHUNK + c], 0, 0)
        )

    return [spec(c) for c in range(CHUNK)]


def whole(shape):
    return pl.BlockSpec(shape, lambda i, *_: (0,) * len(shape))


def local(latents, queries, new_latents, up_proj, lengths, place, block_src, block_slot):
    slot_count = latents.shape[0]
    count = queries.shape[0]
    requests = place.shape[0]
    if lax.axis_size("seq") != 16 or requests > BLOCK or slot_count % CHUNK:
        return move_blocks(
            latents, queries, new_latents, up_proj, lengths, place, block_src, block_slot
        )
    device = lax.axis_index("seq")
    plan = slot_plan(lengths, place, block_src, block_slot, device, slot_count)
    heads = queries.reshape(count, STEPS, HK, GROUP, HD).transpose(0, 2, 1, 3, 4)
    heads = heads.reshape(count, ROWS, HD)
    q_all, up, keys, vals = gather(heads, up_proj, latents)
    q_all = q_all.reshape(requests, ROWS, HD)
    steps = slot_count // CHUNK
    s, m = pl.pallas_call(
        scores_kernel,
        grid_spec=pltpu.PrefetchScalarGridSpec(
            num_scalar_prefetch=3,
            grid=(steps,),
            in_specs=[
                *picked(),
                whole((requests, ROWS, HD)),
            ],
            out_specs=[
                pl.BlockSpec((CHUNK, ROWS, BLOCK), lambda i, *_: (i, 0, 0)),
                whole((ROWS, BLOCK)),
            ],
        ),
        out_shape=[
            jax.ShapeDtypeStruct((slot_count, ROWS, BLOCK), jnp.float32),
            jax.ShapeDtypeStruct((ROWS, BLOCK), jnp.float32),
        ],
        compiler_params=pltpu.CompilerParams(vmem_limit_bytes=48 * 2**20),
    )(*plan, *[keys] * CHUNK, q_all)
    fresh_k = project(new_latents[:, :, :R], up[0]).reshape(count, STEPS, HK, HD)
    fresh_v = project(new_latents[:, :, R:], up[1]).reshape(count, STEPS, HK, HD)
    q_own = heads.reshape(count, HK, STEPS * GROUP, HD)
    fs = jnp.einsum("bgrd,btgd->bgrt", q_own, fresh_k, preferred_element_type=jnp.float32) * SCALE
    ok = jnp.arange(STEPS)[None, :] <= (jnp.arange(STEPS * GROUP) // GROUP)[:, None]
    fs = jnp.where(ok, fs, NEG)
    fm = jnp.max(fs, axis=-1).reshape(count, ROWS)
    first = device * count
    m = m[:, :requests].T
    own = lax.dynamic_slice(m, (first, 0), (count, ROWS))
    m = lax.dynamic_update_slice(m, jnp.maximum(own, fm), (first, 0))
    m = global_max(m)
    own = lax.dynamic_slice(m, (first, 0), (count, ROWS)).reshape(count, HK, STEPS * GROUP)
    m_cols = jnp.pad(m.T, ((0, 0), (0, BLOCK - requests)))
    o, l = pl.pallas_call(
        mix_kernel,
        grid_spec=pltpu.PrefetchScalarGridSpec(
            num_scalar_prefetch=3,
            grid=(steps,),
            in_specs=[
                *picked(),
                pl.BlockSpec((CHUNK, ROWS, BLOCK), lambda i, *_: (i, 0, 0)),
                whole((ROWS, BLOCK)),
            ],
            out_specs=[whole((requests, ROWS, HD)), whole((ROWS, BLOCK))],
            scratch_shapes=[pltpu.VMEM((requests, ROWS, HD), jnp.float32)],
        ),
        out_shape=[
            jax.ShapeDtypeStruct((requests, ROWS, HD), jnp.bfloat16),
            jax.ShapeDtypeStruct((ROWS, BLOCK), jnp.float32),
        ],
        compiler_params=pltpu.CompilerParams(vmem_limit_bytes=48 * 2**20),
    )(*plan, *[vals] * CHUNK, s, m_cols)
    devices = lax.axis_size("seq")
    o, l = scatter(
        o.reshape(devices, count * ROWS, HD), l[:, :requests].T.reshape(devices, count, ROWS)
    )
    fw = jnp.exp(fs - own[..., None])
    l = l.reshape(count, HK, STEPS * GROUP) + jnp.sum(fw, axis=-1)
    o = o.reshape(count, HK, STEPS * GROUP, HD) + jnp.einsum(
        "bgrt,btgd->bgrd", fw.astype(jnp.bfloat16), fresh_v, preferred_element_type=jnp.float32
    )
    o = (o / l[..., None]).astype(jnp.bfloat16)
    o = o.reshape(count, HK, STEPS, GROUP, HD).transpose(0, 2, 1, 3, 4)
    return o.reshape(count, STEPS, HQ * HD)


def solution(mesh):
    return jax.shard_map(
        local,
        mesh=mesh,
        in_specs=(
            P(("groups", "seq"), None, None),
            P(("groups", "seq"), None, None),
            P(("groups", "seq"), None, None),
            P(None, "seq", None),
            P("groups"),
            P("groups"),
            P("groups", None),
            P("groups", None),
        ),
        out_specs=P(("groups", "seq"), None, None),
        check_vma=False,
    )
```
